512 devices in a mesh: dp: 16 (over x, z_lo), tensor: 16 (over y, z_hi), draft: 2 (over core).
Axes of the slice: x: 4, y: 4, z: 16 (z_hi: 4, z_lo: 4; z = z_hi * 4 + z_lo), core: 2. Of those that a mesh axis runs over, the one named last changes fastest.
Arguments:
- rotated_queries: bfloat16 [16, 512, 8192], P('dp', None, ('tensor', 'draft')), may hold values from -6 to 6
- rotated_keys: bfloat16 [16, 512, 1024], P('dp'), may hold values from -6 to 6
- stored_values: bfloat16 [16, 512, 1024], P('dp'), may hold values from -6 to 6
- segment_labels: int32 [16, 512], P('dp'), may hold values from 0 to 7, never falling along the last dimension, each value on 1 to 128 neighbouring positions
- output_gradient: bfloat16 [16, 512, 8192], P('dp', 'draft', 'tensor'), may hold values from -6 to 6
- draft_loss_gradients: bfloat16 [16, 128, 8192], P('dp', 'draft', 'tensor'), may hold values from -6 to 6
- tapped_row_index: int32 [16, 128], P('dp'), may hold values from 0 to 511, as said below
- output_projector: bfloat16 [8192, 8192], P(('tensor', 'draft'), 'dp'), may hold values from -0.0625 to 0.0625
- lower_factor_weight: bfloat16 [8192, 64], P(('tensor', 'draft')), may hold values from -0.0625 to 0.0625
- upper_factor_weight: bfloat16 [64, 8192], P(None, ('tensor', 'draft')), may hold values from -0.0625 to 0.0625
Outputs:
- query_grad: bfloat16 [16, 512, 8192], P('dp', None, ('tensor', 'draft'))
- key_grad: bfloat16 [16, 512, 1024], P('dp', None, ('tensor', 'draft'))
- value_grad: bfloat16 [16, 512, 1024], P('dp', None, ('tensor', 'draft'))
- lower_factor_gradient: float32 [8192, 64], P(('tensor', 'draft'))
- upper_factor_gradient: float32 [64, 8192], P(None, ('tensor', 'draft'))
The draws below stay inside these ranges and needn't reach their ends.
Inputs may be any that keep to these rules, and one draw needn't show every extreme that they name: `tapped_row_index`: within a sequence the 128 rows are distinct and increasing; rows 0 and 511 are always among them.
All inputs are finite; a program needn't handle non-finite values.
Results may differ from the reference program's by a relative error of at most 0.024.
Values may be sent and summed in bfloat16 or wider, within the bound.
No kernel may reach another device: no remote copies, remote signals or barrier semaphores. Data moves between devices by JAX's collectives and lax.ppermute only.
A program may use at most 64 MiB of HBM per device.

```python
import math
import jax
import jax.numpy as jnp
import numpy as np
from jax import lax

MODEL_WIDTH = 8192
QUERY_HEAD_COUNT = 64
KVH = 8
HEAD_WIDTH = 128
ADAPTER_RANK = 64
S = 512
SEGS = 8
SEGMAX = 128
TAPS = 128
BATCH = 16


def draw_rotated_queries(key, part):
    key = jax.random.fold_in(key, 11)
    result = jnp.clip(jax.random.normal(key, (BATCH, S, QUERY_HEAD_COUNT * HEAD_WIDTH)), -5.0, 5.0)
    return result.astype(jnp.bfloat16)


def draw_rotated_keys(key, part):
    key = jax.random.fold_in(key, 12)
    result = jnp.clip(jax.random.normal(key, (BATCH, S, KVH * HEAD_WIDTH)), -5.0, 5.0)
    return result.astype(jnp.bfloat16)


def draw_tapped_row_index(key, part):
    key = jax.random.fold_in(key, 13)
    seq_keys = jax.random.split(key, BATCH)

    def choose_rows(one_key):
        middle_rows = jax.random.permutation(one_key, S - 2)[:TAPS - 2] + 1
        return jnp.sort(middle_rows.astype(jnp.int32))
    middle_rows = jax.vmap(choose_rows)(seq_keys)
    head_row = jnp.zeros((BATCH, 1), jnp.int32)
    tail_row = jnp.full((BATCH, 1), S - 1, jnp.int32)
    return jnp.concatenate([head_row, middle_rows, tail_row], axis=1)


def block_levels(key, extent, cuts, low, high):
    loudness, own = 1.0, jax.random.fold_in(key, 6)
    for dim, shards_of in cuts:
        steps = jnp.exp(jax.random.uniform(jax.random.fold_in(own, dim), (shards_of,), jnp.float32, low / len(cuts), high / len(cuts)))
        loudness = loudness * jnp.repeat(steps, extent[dim] // shards_of).reshape([-1 if axis == dim else 1 for axis in range(len(extent))])
    return loudness


def split_up(number_of, total, reach, skew):
    loads = [(1 << 20) // math.isqrt(rank ** skew) + 1 for rank in range(2, number_of + 1)]
    spare, counts = total - reach - (number_of - 1), [1] * (number_of - 1)
    while spare > 0:
        movable = [i for i in range(number_of - 1) if counts[i] < reach]
        mass, left = sum([loads[i] for i in movable]), spare
        for i in movable:
            more = min(reach - counts[i], max(1, left * loads[i] // mass), spare)
            counts[i] = counts[i] + more
            spare = spare - more
    return np.array([reach] + counts)


def ragged_sizes(own_key, amount, total, reach, slope):
    if amount == 2:
        one = jax.random.randint(own_key, (), max(1, total - reach), min(reach, total - 1) + 1)
        return jnp.stack([one, total - one])
    tallies = jnp.asarray(split_up(amount, total, reach, slope), jnp.int32)
    pairs = (amount - 1) // 2
    source_of, sink = tallies[1:1 + 2 * pairs:2], tallies[2:2 + 2 * pairs:2]
    slack = jnp.minimum(source_of - 1, reach - sink)
    moved = jax.random.randint(jax.random.fold_in(own_key, 1), (pairs,), 0, 1 << 20) % (slack + 1)
    tallies = tallies.at[1:1 + 2 * pairs:2].set(source_of - moved).at[2:2 + 2 * pairs:2].set(sink + moved)
    return tallies[jax.random.permutation(jax.random.fold_in(own_key, 2), amount)]


def noise(stream_key, shape, width, limit, shards=(), kind=jnp.bfloat16):
    array = width * jax.random.normal(stream_key, shape, jnp.float32)
    if shards:
        array = array * block_levels(stream_key, shape, shards, -0.22, 0.18)
    return jnp.clip(array, -limit, limit).astype(kind)


def setup_inputs(seed: int = 0) -> dict:
    streams_of = jax.random.split(jax.random.key(seed), 11)
    return {
        "rotated_queries": draw_rotated_queries(jax.random.fold_in(streams_of[10], 71), 0),
        "rotated_keys": draw_rotated_keys(jax.random.fold_in(streams_of[10], 71), 0),
        "stored_values": noise(streams_of[2], (BATCH, S, KVH * HEAD_WIDTH), 1.0, 6.0, ((0, 16),)),
        "segment_labels": jax.vmap(lambda own: jnp.searchsorted(jnp.cumsum(ragged_sizes(own, SEGS, S, SEGMAX, 1)), jnp.arange(S), side="right"))(jax.random.split(streams_of[3], BATCH)).reshape((BATCH, S)).astype(jnp.int32),
        "output_gradient": noise(streams_of[4], (BATCH, S, MODEL_WIDTH), 1.0, 6.0, ((0, 16), (1, 2), (2, 16))),
        "draft_loss_gradients": noise(streams_of[5], (BATCH, TAPS, MODEL_WIDTH), 1.0, 6.0, ((0, 16), (1, 2), (2, 16))),
        "tapped_row_index": draw_tapped_row_index(jax.random.fold_in(streams_of[10], 71), 0),
        "output_projector": noise(streams_of[7], (QUERY_HEAD_COUNT * HEAD_WIDTH, MODEL_WIDTH), (QUERY_HEAD_COUNT * HEAD_WIDTH) ** -0.5, 0.0625, ((0, 32), (1, 16))),
        "lower_factor_weight": noise(streams_of[8], (QUERY_HEAD_COUNT * HEAD_WIDTH, ADAPTER_RANK), (QUERY_HEAD_COUNT * HEAD_WIDTH) ** -0.5, 0.0625, ((0, 32),)),
        "upper_factor_weight": noise(streams_of[9], (ADAPTER_RANK, MODEL_WIDTH), MODEL_WIDTH ** -0.5, 0.0625, ((1, 32),)),
    }


adapter_scale = 2.0


def sequence_wise(single_query, single_key, single_value, single_segment, single_gradient, single_tapped, single_rows, output_projector, lower_factor_weight, upper_factor_weight):
    group_size = QUERY_HEAD_COUNT // KVH
    seq_len = single_query.shape[0]
    score_scale = HEAD_WIDTH ** -0.5
    summed = single_gradient[single_rows].astype(jnp.float32) + single_tapped.astype(jnp.float32)
    residual_gradient = single_gradient.at[single_rows].set(summed.astype(jnp.bfloat16))
    frozen_gradient = jnp.dot(residual_gradient, output_projector.T, preferred_element_type=jnp.float32)
    query_heads = single_query.reshape(seq_len, QUERY_HEAD_COUNT, HEAD_WIDTH).astype(jnp.float32)
    key_heads = jnp.repeat(single_key.reshape(seq_len, KVH, HEAD_WIDTH), group_size, axis=1).astype(jnp.float32)
    value_heads = jnp.repeat(single_value.reshape(seq_len, KVH, HEAD_WIDTH), group_size, axis=1).astype(jnp.float32)
    positions = jnp.arange(seq_len)
    allowed = (positions[None, :] <= positions[:, None]) & (single_segment[:, None] == single_segment[None, :])
    scores = jnp.einsum("ihd,jhd->hij", query_heads, key_heads) * score_scale
    scores = jnp.where(allowed[None], scores, -jnp.inf)
    probs_full = jax.nn.softmax(scores, axis=-1)
    probs_half = lax.optimization_barrier(probs_full.astype(jnp.bfloat16)).astype(jnp.float32)
    attn_out = jnp.einsum("hij,jhd->ihd", probs_half, value_heads).astype(jnp.bfloat16)
    attn_wide = lax.optimization_barrier(attn_out).astype(jnp.float32)
    output_flattened = attn_out.reshape(seq_len, QUERY_HEAD_COUNT * HEAD_WIDTH)
    adapter_inner = jnp.dot(output_flattened, lower_factor_weight, preferred_element_type=jnp.float32).astype(jnp.bfloat16)
    adapter_gradient = jnp.dot(residual_gradient, upper_factor_weight.T, preferred_element_type=jnp.float32).astype(jnp.bfloat16)
    head_gradient = (frozen_gradient + adapter_scale * jnp.dot(adapter_gradient, lower_factor_weight.T, preferred_element_type=jnp.float32)).astype(jnp.bfloat16)
    grad_heads = lax.optimization_barrier(head_gradient).astype(jnp.float32).reshape(seq_len, QUERY_HEAD_COUNT, HEAD_WIDTH)
    value_full = jnp.einsum("hij,ihd->jhd", probs_half, grad_heads)
    prob_grad = jnp.einsum("ihd,jhd->hij", grad_heads, value_heads)
    row_terms = jnp.einsum("ihd,ihd->hi", grad_heads, attn_wide)
    score_grad = (probs_full * (prob_grad - row_terms[:, :, None])).astype(jnp.bfloat16)
    score_grad = lax.optimization_barrier(score_grad).astype(jnp.float32)
    query_grad = (score_scale * jnp.einsum("hij,jhd->ihd", score_grad, key_heads)).astype(jnp.bfloat16)
    key_full = score_scale * jnp.einsum("hij,ihd->jhd", score_grad, query_heads)
    key_grad = key_full.reshape(seq_len, KVH, group_size, HEAD_WIDTH).sum(axis=2).astype(jnp.bfloat16)
    value_grad = value_full.reshape(seq_len, KVH, group_size, HEAD_WIDTH).sum(axis=2).astype(jnp.bfloat16)
    lower_factor_gradient = adapter_scale * jnp.dot(output_flattened.T, adapter_gradient, preferred_element_type=jnp.float32)
    upper_factor_gradient = adapter_scale * jnp.dot(adapter_inner.T, residual_gradient, preferred_element_type=jnp.float32)
    return (query_grad.reshape(seq_len, QUERY_HEAD_COUNT * HEAD_WIDTH), key_grad.reshape(seq_len, KVH * HEAD_WIDTH),
            value_grad.reshape(seq_len, KVH * HEAD_WIDTH), lower_factor_gradient, upper_factor_gradient)


def reference(rotated_queries, rotated_keys, stored_values, segment_labels, output_gradient, draft_loss_gradients, tapped_row_index, output_projector, lower_factor_weight, upper_factor_weight):
    def one_index(sequence_index):
        return sequence_wise(rotated_queries[sequence_index], rotated_keys[sequence_index], stored_values[sequence_index],
                            segment_labels[sequence_index], output_gradient[sequence_index], draft_loss_gradients[sequence_index],
                            tapped_row_index[sequence_index], output_projector, lower_factor_weight, upper_factor_weight)

    results = lax.map(one_index, jnp.arange(BATCH))
    lower_factor_gradient = jnp.sum(results[3], axis=0) / BATCH
    upper_factor_gradient = jnp.sum(results[4], axis=0) / BATCH
    return results[0], results[1], results[2], lower_factor_gradient, upper_factor_gradient
```

```python
import jax
import jax.numpy as jnp
from jax import lax
from jax.experimental import pallas as pl
from jax.experimental.pallas import tpu as pltpu
from jax.sharding import PartitionSpec as P

QUERY_HEAD_COUNT = 64
KVH = 8
HEAD_WIDTH = 128
SIDE = 4

adapter_scale = 2.0

F32, BF16 = jnp.float32, jnp.bfloat16
NT = (((1,), (1,)), ((), ()))
TN = (((0,), (0,)), ((), ()))


def high_shift(array, axis, k):
    pairs = [(i * SIDE + j, (i + k) % SIDE * SIDE + j) for i in range(SIDE) for j in range(SIDE)]
    return lax.ppermute(array, axis, pairs)


def low_shift(array, axis, k):
    pairs = [(i * SIDE + j, i * SIDE + (j + k) % SIDE) for i in range(SIDE) for j in range(SIDE)]
    return lax.ppermute(array, axis, pairs)


def swapped(array, axis, mask):
    return lax.ppermute(array, axis, [(i, i ^ mask) for i in range(lax.axis_size(axis))])


def halves(array, upper):
    n = array.shape[0] // 2
    low, high = array[:n], array[n:]
    return jnp.where(upper, high, low), jnp.where(upper, low, high)


def scatter_step(array, axis, mask, upper):
    keep, give = halves(array, upper)
    return keep + swapped(give, axis, mask)


def gather_step(array, axis, mask, upper):
    other = swapped(array, axis, mask)
    return jnp.concatenate([jnp.where(upper, other, array), jnp.where(upper, array, other)], axis=0)


def frozen_kernel(order_ref, *refs):
    pieces, slab, mine, other = refs[:16], refs[16], refs[17], refs[18]
    n = mine.shape[1]
    total = None
    for i, piece in enumerate(pieces):
        term = lax.dot_general(piece[...], slab[order_ref[i]], NT, preferred_element_type=F32)
        total = term if total is None else total + term
    mine[...] = total[:, :n]
    other[...] = total[:, n:]


def frozen_product(order, pieces, slab):
    rows, cols = pieces[0].shape[0], slab.shape[1] // 2
    return pl.pallas_call(
        frozen_kernel,
        out_shape=(jax.ShapeDtypeStruct((rows, cols), F32),) * 2,
        in_specs=[pl.BlockSpec(memory_space=pltpu.SMEM)]
        + [pl.BlockSpec(memory_space=pltpu.VMEM)] * 17,
        out_specs=(pl.BlockSpec(memory_space=pltpu.VMEM),) * 2,
        compiler_params=pltpu.CompilerParams(vmem_limit_bytes=40 * 1024 * 1024),
        name="frozen",
    )(order, *pieces, slab)


def on_device(
    rotated_queries,
    rotated_keys,
    stored_values,
    segment_labels,
    output_gradient,
    draft_loss_gradients,
    tapped_row_index,
    output_projector,
    lower_factor_weight,
    upper_factor_weight,
):
    seq_len = rotated_queries.shape[1]
    head_size = HEAD_WIDTH
    heads_dev = rotated_queries.shape[2] // head_size
    group_size = QUERY_HEAD_COUNT // KVH
    score_scale = head_size ** (-0.5)
    core = lax.axis_index("draft")
    tensor = lax.axis_index("tensor")
    dp = lax.axis_index("dp")
    upper_core = core == 1
    rank_index = tensor * 2 + core
    kv_head = rank_index * heads_dev // group_size
    tapped = tapped_row_index[0]
    width = output_projector.shape[1] // 2
    rank = lower_factor_weight.shape[1]

    local = jnp.concatenate([output_gradient[0], draft_loss_gradients[0], output_projector], axis=0)
    low, high = local[:, :width], local[:, width:]
    own = jnp.where(upper_core, high, low)
    came = swapped(jnp.where(upper_core, low, high), "draft", 1)
    nr, nt = output_gradient.shape[1], draft_loss_gradients.shape[1]
    first, second = jnp.where(upper_core, came, own), jnp.where(upper_core, own, came)
    slab_own = jnp.concatenate([own[nr + nt :], came[nr + nt :]], axis=0)
    slab = lax.all_gather(slab_own, "dp", axis=0)
    rows = jnp.concatenate([first[:nr], second[:nr]], axis=0)
    taps = jnp.concatenate([first[nr : nr + nt], second[nr : nr + nt]], axis=0)
    hit = (jnp.arange(seq_len)[:, None] == tapped[None, :]).astype(BF16)
    spread = jnp.dot(hit, taps, preferred_element_type=F32)
    residual = (rows.astype(F32) + spread).astype(BF16)

    z1, z3, z2 = (low_shift(residual, "tensor", k) for k in (1, 3, 2))
    pieces = {(0, 0): residual, (0, 1): z1, (0, 3): z3, (0, 2): z2}
    near = jnp.concatenate([z1, z3], axis=0)
    for k in (1, 3, 2):
        pieces[k, 0] = high_shift(residual, "tensor", k)
    for k in (1, 3, 2):
        both = high_shift(near, "tensor", k)
        pieces[k, 1], pieces[k, 3] = both[:seq_len], both[seq_len:]
    for k in (1, 3, 2):
        pieces[k, 2] = high_shift(z2, "tensor", k)
    keys = sorted(pieces)
    order = jnp.stack(
        [(tensor // SIDE - a) % SIDE * SIDE + (tensor % SIDE - b) % SIDE for a, b in keys]
    ).astype(jnp.int32)

    query_heads = rotated_queries[0].reshape(seq_len, heads_dev, head_size)
    key_head = lax.dynamic_slice_in_dim(rotated_keys[0], kv_head * head_size, head_size, 1)
    value_head = lax.dynamic_slice_in_dim(stored_values[0], kv_head * head_size, head_size, 1)
    positions = jnp.arange(seq_len)
    segments_row = segment_labels[0]
    allowed = (positions[None, :] <= positions[:, None]) & (
        segments_row[:, None] == segments_row[None, :]
    )
    scores = (
        jnp.einsum("ihd,jd->hij", query_heads, key_head, preferred_element_type=F32) * score_scale
    )
    scores = jnp.where(allowed[None], scores, -jnp.inf)
    probs_full = jax.nn.softmax(scores, axis=-1)
    probs_half = probs_full.astype(BF16)
    attn_out = jnp.einsum("hij,jd->ihd", probs_half, value_head, preferred_element_type=F32).astype(
        BF16
    )
    output_flattened = attn_out.reshape(seq_len, heads_dev * head_size)

    inner_piece = jnp.dot(output_flattened, lower_factor_weight, preferred_element_type=F32)
    adapter_piece = lax.dot_general(residual, upper_factor_weight, NT, preferred_element_type=F32)
    sums = jnp.concatenate([inner_piece, adapter_piece], axis=1)
    sums = scatter_step(sums, "draft", 1, upper_core)
    sums = scatter_step(sums, "tensor", 4, tensor & 4 != 0)
    sums = scatter_step(sums, "tensor", 8, tensor & 8 != 0)
    sums = sums + swapped(sums, "tensor", 1)
    sums = sums + swapped(sums, "tensor", 2)
    sums = sums.astype(BF16)
    sums = gather_step(sums, "tensor", 8, tensor & 8 != 0)
    sums = gather_step(sums, "tensor", 4, tensor & 4 != 0)
    sums = gather_step(sums, "draft", 1, upper_core)
    adapter_inner, adapter_gradient = sums[:, :rank], sums[:, rank:]

    lower_piece = lax.dot_general(adapter_gradient, output_flattened, TN, preferred_element_type=F32)
    upper_piece = lax.dot_general(adapter_inner, residual, TN, preferred_element_type=F32)
    factor = jnp.concatenate([lower_piece, upper_piece], axis=0)
    factor = scatter_step(factor, "dp", 4, dp & 4 != 0)
    factor = scatter_step(factor, "dp", 8, dp & 8 != 0)
    factor = factor + swapped(factor, "dp", 1)
    factor = factor + swapped(factor, "dp", 2)
    factor = factor * (adapter_scale / lax.axis_size("dp"))
    factor = gather_step(factor, "dp", 8, dp & 8 != 0)
    factor = gather_step(factor, "dp", 4, dp & 4 != 0)
    lower_gradient, upper_gradient = factor[:rank].T, factor[rank:]

    part_mine, part_other = frozen_product(order, [pieces[k] for k in keys], slab)
    frozen_gradient = part_mine + swapped(part_other, "draft", 1)
    adapter_backward = lax.dot_general(
        adapter_gradient, lower_factor_weight, NT, preferred_element_type=F32
    )
    head_gradient = (frozen_gradient + adapter_scale * adapter_backward).astype(BF16)

    grad_heads = head_gradient.reshape(seq_len, heads_dev, head_size)
    value_part = jnp.einsum("hij,ihd->jd", probs_half, grad_heads, preferred_element_type=F32)
    prob_grad = jnp.einsum("ihd,jd->hij", grad_heads, value_head, preferred_element_type=F32)
    row_terms = jnp.einsum("ihd,ihd->hi", grad_heads, attn_out, preferred_element_type=F32)
    score_grad = (probs_full * (prob_grad - row_terms[:, :, None])).astype(BF16)
    query_grad = score_scale * jnp.einsum(
        "hij,jd->ihd", score_grad, key_head, preferred_element_type=F32
    )
    query_grad = query_grad.astype(BF16).reshape(1, seq_len, heads_dev * head_size)
    key_part = score_scale * jnp.einsum(
        "hij,ihd->jd", score_grad, query_heads, preferred_element_type=F32
    )
    combined = jnp.stack([key_part, value_part], axis=1).reshape(
        seq_len, 2, 2, 2, head_size // 4
    )
    keep = jnp.where(upper_core, combined[:, :, :, 1], combined[:, :, :, 0])
    give = jnp.where(upper_core, combined[:, :, :, 0], combined[:, :, :, 1])
    combined = keep + swapped(give, "draft", 1)
    upper_chip = tensor & 1 == 1
    keep = jnp.where(upper_chip, combined[:, :, 1], combined[:, :, 0])
    give = jnp.where(upper_chip, combined[:, :, 0], combined[:, :, 1])
    combined = keep + swapped(give, "tensor", 1)
    key_grad = combined[:, 0].astype(BF16)[None]
    value_grad = combined[:, 1].astype(BF16)[None]
    return (query_grad, key_grad, value_grad, lower_gradient, upper_gradient)


def solution(mesh):
    in_specs = (
        P("dp", None, ("tensor", "draft")),
        P("dp", None, None),
        P("dp", None, None),
        P("dp", None),
        P("dp", "draft", "tensor"),
        P("dp", "draft", "tensor"),
        P("dp", None),
        P(("tensor", "draft"), "dp"),
        P(("tensor", "draft"), None),
        P(None, ("tensor", "draft")),
    )
    out_specs = (
        P("dp", None, ("tensor", "draft")),
        P("dp", None, ("tensor", "draft")),
        P("dp", None, ("tensor", "draft")),
        P(("tensor", "draft"), None),
        P(None, ("tensor", "draft")),
    )
    return jax.shard_map(
        on_device, mesh=mesh, in_specs=in_specs, out_specs=out_specs, check_vma=False
    )
```

```python
import functools

import jax
import jax.numpy as jnp
from jax import lax
from jax.experimental import pallas as pl
from jax.experimental.pallas import tpu as pltpu
from jax.sharding import PartitionSpec as P

QUERY_HEAD_COUNT = 64
KVH = 8
HEAD_WIDTH = 128
SIDE = 4

adapter_scale = 2.0

F32, BF16 = jnp.float32, jnp.bfloat16
NT = (((1,), (1,)), ((), ()))
TN = (((0,), (0,)), ((), ()))


AXES = ("dp", "tensor", "draft")
Z_SHIFT, Z_MASK = (0, 1, 3, 2), (0, 1, 2, 3)


def moved(array, residual_to, slab_to):
    n_dp, n_tensor = lax.axis_size("dp"), lax.axis_size("tensor")
    pairs = []
    for d in range(n_dp):
        for t in range(n_tensor):
            at = (d * n_tensor + t) * 2
            pairs.append((at, (d * n_tensor + residual_to(t)) * 2))
            pairs.append((at + 1, (slab_to(d) * n_tensor + t) * 2 + 1))
    return lax.ppermute(array, AXES, pairs)


def far_move(array, k):
    step = lambda i: (i + k * SIDE) % (SIDE * SIDE)
    return moved(array, step, step)


def near_move(array, stage):
    ahead = lambda t: t // SIDE * SIDE + (t + Z_SHIFT[stage]) % SIDE
    return moved(array, ahead, lambda d: d ^ Z_MASK[stage])


def swapped(array, axis, mask):
    return lax.ppermute(array, axis, [(i, i ^ mask) for i in range(lax.axis_size(axis))])


def halves(array, upper):
    n = array.shape[0] // 2
    low, high = array[:n], array[n:]
    return jnp.where(upper, high, low), jnp.where(upper, low, high)


def scatter_step(array, axis, mask, upper):
    keep, give = halves(array, upper)
    return keep + swapped(give, axis, mask)


def gather_step(array, axis, mask, upper):
    other = swapped(array, axis, mask)
    return jnp.concatenate([jnp.where(upper, other, array), jnp.where(upper, array, other)], axis=0)


def after(array, *earlier):
    return lax.optimization_barrier((array, *earlier))[0]


def pack_kernel(core_ref, rows_ref, taps_ref, slab_ref, give_ref):
    n = rows_ref.shape[0]

    @pl.when(core_ref[0] == 0)
    def _():
        give_ref[:n] = slab_ref[...]

    @pl.when(core_ref[0] == 1)
    def _():
        give_ref[:n] = rows_ref[...]

    give_ref[n:] = taps_ref[...]


def pack(core, rows, taps, slab):
    return pl.pallas_call(
        pack_kernel,
        out_shape=jax.ShapeDtypeStruct((rows.shape[0] + taps.shape[0], rows.shape[1]), BF16),
        in_specs=[pl.BlockSpec(memory_space=pltpu.SMEM)]
        + [pl.BlockSpec(memory_space=pltpu.VMEM)] * 3,
        out_specs=pl.BlockSpec(memory_space=pltpu.VMEM),
        name="pack",
    )(core, rows, taps, slab)


def blend_kernel(core_ref, tapped_ref, rows_ref, taps_ref, slab_ref, came_ref, block_ref, give_ref):
    n, n_taps = rows_ref.shape[0], taps_ref.shape[0]
    half = give_ref.shape[1]

    @pl.when(core_ref[0] == 0)
    def _():
        taps = jnp.concatenate([taps_ref[...], came_ref[n:]], axis=0)
        place = lax.broadcasted_iota(jnp.int32, (2 * n, 2 * n_taps), 0)
        hit = jnp.where(place == tapped_ref[...], 1.0, 0.0).astype(BF16)
        spread = jnp.dot(hit, taps, preferred_element_type=F32)
        block_ref[:n] = (rows_ref[...].astype(F32) + spread[:n]).astype(BF16)
        block_ref[n:] = (came_ref[:n].astype(F32) + spread[n:]).astype(BF16)
        give_ref[...] = block_ref[:, half:]

    @pl.when(core_ref[0] == 1)
    def _():
        block_ref[:n] = came_ref[:n]
        block_ref[n:] = slab_ref[...]
        give_ref[...] = block_ref[:, :half]


def blend(core, tapped, rows, taps, slab, came):
    n, width = rows.shape
    return pl.pallas_call(
        blend_kernel,
        out_shape=(
            jax.ShapeDtypeStruct((2 * n, width), BF16),
            jax.ShapeDtypeStruct((2 * n, width // 2), BF16),
        ),
        in_specs=[pl.BlockSpec(memory_space=pltpu.SMEM)]
        + [pl.BlockSpec(memory_space=pltpu.VMEM)] * 5,
        out_specs=(pl.BlockSpec(memory_space=pltpu.VMEM),) * 2,
        name="blend",
    )(core, tapped, rows, taps, slab, came)


def give_half(core, arrays):
    half = arrays[0].shape[1] // 2
    return jnp.concatenate(
        [jnp.where(core == 1, a[:, :half], a[:, half:]) for a in arrays], axis=0
    )


def frozen_kernel(n_held, sizes, core_ref, order_ref, *refs):
    n = len(sizes)
    sources, (mine, other, own, came, sems) = refs[:n], refs[n:]
    rows, cols = mine.shape
    width = own.shape[1]
    blocks = own.shape[0] // rows
    columns = pl.ds(pl.multiple_of(core_ref[0] * width, width), width)
    copies, at = [], 0
    for i, size in enumerate(sizes):
        if i == n_held:
            at = 0
        if i < n_held:
            source, target = sources[i].at[:, columns], own.at[pl.ds(at, size)]
        else:
            source, target = sources[i], came.at[pl.ds(at, size)]
        copies.append(pltpu.make_async_copy(source, target, sems.at[i]))
        copies[-1].start()
        at += size
    for copy in copies:
        copy.wait()

    def matched(i):
        return came[pl.ds(pl.multiple_of(order_ref[i] * rows, rows), rows)]

    def held(i):
        return own[i * rows : (i + 1) * rows]

    def product(left, right):
        return lax.dot_general(left, right, NT, preferred_element_type=F32)

    @pl.when(core_ref[0] == 0)
    def _():
        total = product(held(0), matched(0))
        for i in range(1, blocks):
            total = total + product(held(i), matched(i))
        mine[...] = total[:, :cols]
        other[...] = total[:, cols:]

    @pl.when(core_ref[0] == 1)
    def _():
        total = product(matched(0), held(0))
        for i in range(1, blocks):
            total = total + product(matched(i), held(i))
        mine[...] = total[:, cols:]
        other[...] = total[:, :cols]


def frozen_product(core, order, own, came, rows):
    arrays = (*own, *came)
    sizes = tuple(a.shape[0] for a in arrays)
    width = came[0].shape[1]
    held = pltpu.VMEM((sum(a.shape[0] for a in own), width), BF16)
    return pl.pallas_call(
        functools.partial(frozen_kernel, len(own), sizes),
        out_shape=(jax.ShapeDtypeStruct((rows, rows // 2), F32),) * 2,
        in_specs=[pl.BlockSpec(memory_space=pltpu.SMEM)] * 2
        + [pl.BlockSpec(memory_space=pl.ANY)] * len(arrays),
        out_specs=(pl.BlockSpec(memory_space=pltpu.VMEM),) * 2,
        scratch_shapes=[held, held, pltpu.SemaphoreType.DMA((len(arrays),))],
        compiler_params=pltpu.CompilerParams(vmem_limit_bytes=56 * 1024 * 1024),
        name="frozen",
    )(core, order, *arrays)


def block_order(core, dp, tensor):
    stage = jnp.array([0] * 4 + [1, 2] * 4 + [3] * 4, jnp.int32)
    step = jnp.array([0, 1, 2, 3, 0, 0, 1, 1, 2, 2, 3, 3, 0, 1, 2, 3], jnp.int32)
    shift = jnp.where(stage == 2, 3, jnp.where(stage == 3, 2, stage))
    first = core == 0
    high = jnp.where(first, tensor // SIDE - step, dp // SIDE - step) % SIDE
    low = jnp.where(first, (tensor - shift) % SIDE, (dp % SIDE) ^ stage)
    their_step = jnp.where(first, dp // SIDE - high, tensor // SIDE - high) % SIDE
    back = (tensor - low) % SIDE
    back = jnp.where(back == 2, 3, jnp.where(back == 3, 2, back))
    their_stage = jnp.where(first, (dp % SIDE) ^ low, back)
    middle = 3 + their_stage + 2 * their_step
    return jnp.where(
        their_stage == 0, their_step, jnp.where(their_stage == 3, 12 + their_step, middle)
    )


def on_device(
    rotated_queries,
    rotated_keys,
    stored_values,
    segment_labels,
    output_gradient,
    draft_loss_gradients,
    tapped_row_index,
    output_projector,
    lower_factor_weight,
    upper_factor_weight,
):
    seq_len = rotated_queries.shape[1]
    head_size = HEAD_WIDTH
    heads_dev = rotated_queries.shape[2] // head_size
    group_size = QUERY_HEAD_COUNT // KVH
    score_scale = head_size ** (-0.5)
    core = lax.axis_index("draft")
    tensor = lax.axis_index("tensor")
    dp = lax.axis_index("dp")
    upper_core = core == 1
    rank_index = tensor * 2 + core
    kv_head = rank_index * heads_dev // group_size
    width = output_projector.shape[1] // 2
    rank = lower_factor_weight.shape[1]

    core_ref = core.reshape(1)
    rows, taps = output_gradient[0], draft_loss_gradients[0]
    came = swapped(pack(core_ref, rows, taps, output_projector), "draft", 1)
    block, give = blend(core_ref, tapped_row_index, rows, taps, output_projector, came)
    came_own = swapped(give, "draft", 1)
    residual = jnp.where(upper_core, came_own, block[:, :width])

    z1, z2 = near_move(block, 1), near_move(block, 2)
    own_far = [far_move(block, k) for k in (1, 2, 3)]
    z3 = near_move(after(block, z1, z2, *own_far), 3)
    near = jnp.concatenate([z1, z2], axis=0)
    near_far = [far_move(near, k) for k in (1, 2, 3)]
    came_far = swapped(after(give_half(core, own_far), z1, z2), "draft", 1)
    last_far = [far_move(z3, k) for k in (1, 2, 3)]
    came_near = swapped(after(give_half(core, [z1, z2, *near_far]), z3), "draft", 1)
    came_last = swapped(give_half(core, [z3, *last_far]), "draft", 1)
    order = block_order(core, dp, tensor)

    query_heads = rotated_queries[0].reshape(seq_len, heads_dev, head_size)
    key_head = lax.dynamic_slice_in_dim(rotated_keys[0], kv_head * head_size, head_size, 1)
    value_head = lax.dynamic_slice_in_dim(stored_values[0], kv_head * head_size, head_size, 1)
    positions = jnp.arange(seq_len)
    segments_row = segment_labels[0]
    allowed = (positions[None, :] <= positions[:, None]) & (
        segments_row[:, None] == segments_row[None, :]
    )
    scores = (
        jnp.einsum("ihd,jd->hij", query_heads, key_head, preferred_element_type=F32) * score_scale
    )
    scores = jnp.where(allowed[None], scores, -jnp.inf)
    probs_full = jax.nn.softmax(scores, axis=-1)
    probs_half = probs_full.astype(BF16)
    attn_out = jnp.einsum("hij,jd->ihd", probs_half, value_head, preferred_element_type=F32).astype(
        BF16
    )
    output_flattened = attn_out.reshape(seq_len, heads_dev * head_size)

    inner_piece = jnp.dot(output_flattened, lower_factor_weight, preferred_element_type=F32)
    adapter_piece = lax.dot_general(residual, upper_factor_weight, NT, preferred_element_type=F32)
    sums = jnp.concatenate([inner_piece, adapter_piece], axis=1)
    sums = scatter_step(after(sums, *own_far), "draft", 1, upper_core)
    sums = scatter_step(after(sums, z1, z2), "tensor", 4, tensor & 4 != 0)
    sums = scatter_step(sums, "tensor", 8, tensor & 8 != 0)
    sums = after(sums, z3)
    sums = sums + swapped(sums, "tensor", 1)
    sums = sums + swapped(sums, "tensor", 2)
    sums = sums.astype(BF16)
    sums = gather_step(sums, "tensor", 8, tensor & 8 != 0)
    sums = gather_step(sums, "tensor", 4, tensor & 4 != 0)
    sums = gather_step(sums, "draft", 1, upper_core)
    adapter_inner, adapter_gradient = sums[:, :rank], sums[:, rank:]

    lower_piece = lax.dot_general(adapter_gradient, output_flattened, TN, preferred_element_type=F32)
    upper_piece = lax.dot_general(adapter_inner, residual, TN, preferred_element_type=F32)
    factor = jnp.concatenate([lower_piece, upper_piece], axis=0)
    factor = after(factor, *near_far)
    for mask in (4, 8, 1, 2):
        factor = factor + swapped(factor, "dp", mask)
    factor = factor * (adapter_scale / lax.axis_size("dp"))
    lower_gradient, upper_gradient = factor[:rank].T, factor[rank:]

    part_mine, part_other = frozen_product(
        core_ref,
        order,
        [block, *own_far, z1, z2, *near_far, z3, *last_far],
        [came_own, came_far, came_near, came_last],
        seq_len,
    )
    frozen_gradient = part_mine + swapped(part_other, "draft", 1)
    adapter_backward = lax.dot_general(
        adapter_gradient, lower_factor_weight, NT, preferred_element_type=F32
    )
    head_gradient = (frozen_gradient + adapter_scale * adapter_backward).astype(BF16)

    grad_heads = head_gradient.reshape(seq_len, heads_dev, head_size)
    value_part = jnp.einsum("hij,ihd->jd", probs_half, grad_heads, preferred_element_type=F32)
    prob_grad = jnp.einsum("ihd,jd->hij", grad_heads, value_head, preferred_element_type=F32)
    row_terms = jnp.einsum("ihd,ihd->hi", grad_heads, attn_out, preferred_element_type=F32)
    score_grad = (probs_full * (prob_grad - row_terms[:, :, None])).astype(BF16)
    query_grad = score_scale * jnp.einsum(
        "hij,jd->ihd", score_grad, key_head, preferred_element_type=F32
    )
    query_grad = query_grad.astype(BF16).reshape(1, seq_len, heads_dev * head_size)
    key_part = score_scale * jnp.einsum(
        "hij,ihd->jd", score_grad, query_heads, preferred_element_type=F32
    )
    combined = jnp.stack([key_part, value_part], axis=1).reshape(
        seq_len, 2, 2, 2, head_size // 4
    )
    keep = jnp.where(upper_core, combined[:, :, :, 1], combined[:, :, :, 0])
    give = jnp.where(upper_core, combined[:, :, :, 0], combined[:, :, :, 1])
    combined = keep + swapped(give, "draft", 1)
    upper_chip = tensor & 1 == 1
    keep = jnp.where(upper_chip, combined[:, :, 1], combined[:, :, 0])
    give = jnp.where(upper_chip, combined[:, :, 0], combined[:, :, 1])
    combined = keep + swapped(give.astype(BF16), "tensor", 1).astype(F32)
    key_grad = combined[:, 0].astype(BF16)[None]
    value_grad = combined[:, 1].astype(BF16)[None]
    return (query_grad, key_grad, value_grad, lower_gradient, upper_gradient)


def solution(mesh):
    in_specs = (
        P("dp", None, ("tensor", "draft")),
        P("dp", None, None),
        P("dp", None, None),
        P("dp", None),
        P("dp", "draft", "tensor"),
        P("dp", "draft", "tensor"),
        P("dp", None),
        P(("tensor", "draft"), "dp"),
        P(("tensor", "draft"), None),
        P(None, ("tensor", "draft")),
    )
    out_specs = (
        P("dp", None, ("tensor", "draft")),
        P("dp", None, ("tensor", "draft")),
        P("dp", None, ("tensor", "draft")),
        P(("tensor", "draft"), None),
        P(None, ("tensor", "draft")),
    )
    return jax.shard_map(
        on_device, mesh=mesh, in_specs=in_specs, out_specs=out_specs, check_vma=False
    )
```

```python
import functools

import jax
import jax.numpy as jnp
from jax import lax
from jax.experimental import pallas as pl
from jax.experimental.pallas import tpu as pltpu
from jax.sharding import PartitionSpec as P

QUERY_HEAD_COUNT = 64
KVH = 8
HEAD_WIDTH = 128
SIDE = 4
SEGMENT_MOST = 128
JOIN_WEIGHT = 96 << 20

adapter_scale = 2.0

F32, BF16 = jnp.float32, jnp.bfloat16
NT = (((1,), (1,)), ((), ()))
TN = (((0,), (0,)), ((), ()))


AXES = ("dp", "tensor", "draft")


def moved(array, residual_to, slab_to):
    n_dp, n_tensor = lax.axis_size("dp"), lax.axis_size("tensor")
    pairs = []
    for d in range(n_dp):
        for t in range(n_tensor):
            at = (d * n_tensor + t) * 2
            pairs.append((at, (d * n_tensor + residual_to(t)) * 2))
            pairs.append((at + 1, (slab_to(d) * n_tensor + t) * 2 + 1))
    return lax.ppermute(array, AXES, pairs)


def spread(stacked, axes, groups):
    return lax.all_to_all(stacked, axes, 0, 0, axis_index_groups=groups, tiled=True)


def high_groups():
    return [[i * SIDE + j for i in range(SIDE)] for j in range(SIDE)]


def far_groups():
    n_dp, n_tensor = lax.axis_size("dp"), lax.axis_size("tensor")
    groups = []
    for one in high_groups():
        groups += [[(d * n_tensor + t) * 2 for t in one] for d in range(n_dp)]
        groups += [[(d * n_tensor + t) * 2 + 1 for d in one] for t in range(n_tensor)]
    return groups


def far_move(array, k):
    step = lambda i: (i + k * SIDE) % (SIDE * SIDE)
    return moved(array, step, step)


def near_move(array, shift, mask):
    ahead = lambda t: t // SIDE * SIDE + (t + shift) % SIDE
    return moved(array, ahead, lambda d: d ^ mask)


def first_swapped(array, mask):
    n = lax.axis_size("dp") * lax.axis_size("tensor")
    return lax.ppermute(array, AXES, [(2 * i, 2 * (i ^ mask)) for i in range(n)])


def swapped(array, axis, mask):
    return lax.ppermute(array, axis, [(i, i ^ mask) for i in range(lax.axis_size(axis))])


def after(array, *earlier):
    return lax.optimization_barrier((array, *earlier))[0]


def blend_kernel(
    place_ref, tapped_ref, rows_ref, taps_ref, upper_ref, slab_ref, came_ref, inner_ref,
    block_ref, sums_ref, stack_ref,
):
    n, n_taps, rank = rows_ref.shape[0], taps_ref.shape[0], upper_ref.shape[0]
    width = upper_ref.shape[1]
    at_upper = n + n_taps
    at_inner = at_upper + rank // 2

    @pl.when(place_ref[0] == 0)
    def _():
        taps = jnp.concatenate([taps_ref[...], came_ref[n:at_upper]], axis=0)
        place = lax.broadcasted_iota(jnp.int32, (2 * n, 2 * n_taps), 0)
        hit = jnp.where(place == tapped_ref[...], 1.0, 0.0).astype(BF16)
        spread = jnp.dot(hit, taps, preferred_element_type=F32)
        block_ref[:n] = (rows_ref[...].astype(F32) + spread[:n]).astype(BF16)
        block_ref[n:] = (came_ref[:n].astype(F32) + spread[n:]).astype(BF16)
        upper = came_ref[at_upper:at_inner]
        upper = jnp.concatenate([upper[:, :width], upper[:, width:]], axis=0)
        lora = lax.dot_general(
            block_ref[:, :width], upper_ref[...], NT, preferred_element_type=F32
        ) + lax.dot_general(block_ref[:, width:], upper, NT, preferred_element_type=F32)
        inner = came_ref[at_inner:].astype(F32)
        inner = [inner[:, i * rank : (i + 1) * rank] for i in range(inner.shape[1] // rank)]
        inner = inner_ref[...] + jnp.concatenate(inner, axis=0)
        sums_ref[...] = jnp.concatenate([inner, lora], axis=1)

    @pl.when(place_ref[0] == 1)
    def _():
        block_ref[:n] = came_ref[:n]
        block_ref[n:] = slab_ref[...]
        sums_ref[...] = jnp.zeros_like(sums_ref)

    quarter = 2 * n // SIDE
    step = stack_ref.shape[0] // SIDE
    for i in range(SIDE):
        at = i * step
        stack_ref[at : at + 2 * n] = block_ref[...]
        share = sums_ref[i * quarter : (i + 1) * quarter].astype(BF16)
        stack_ref[at + 2 * n : at + step] = jnp.concatenate(
            jnp.split(share, SIDE, axis=0), axis=1
        )


def blend(place, tapped, rows, taps, upper, slab, came, inner):
    n, width = rows.shape
    ride = 2 * n // SIDE * 2 * upper.shape[0] // width
    vmem = pl.BlockSpec(memory_space=pltpu.VMEM)
    return pl.pallas_call(
        blend_kernel,
        out_shape=(
            jax.ShapeDtypeStruct((2 * n, width), BF16),
            jax.ShapeDtypeStruct((2 * n, 2 * upper.shape[0]), F32),
            jax.ShapeDtypeStruct((SIDE * (2 * n + ride), width), BF16),
        ),
        in_specs=[pl.BlockSpec(memory_space=pltpu.SMEM)] + [vmem] * 7,
        out_specs=(vmem,) * 3,
        name="blend",
    )(place, tapped, rows, taps, upper, slab, came, inner)


def widened(array, n):
    return jnp.concatenate(jnp.split(array, n, axis=0), axis=1)


def narrowed(array, n):
    return jnp.concatenate(jnp.split(array, n, axis=1), axis=0)


def joined_kernel(low_ref, high_ref, out_ref):
    n = low_ref.shape[0]
    out_ref[:n] = low_ref[...]
    out_ref[n:] = high_ref[...]


def joined(low, high):
    n, width = low.shape
    vmem = pl.BlockSpec(memory_space=pltpu.VMEM)
    return pl.pallas_call(
        joined_kernel,
        out_shape=jax.ShapeDtypeStruct((2 * n, width), BF16),
        in_specs=[vmem] * 2,
        out_specs=vmem,
        cost_estimate=pl.CostEstimate(flops=0, bytes_accessed=JOIN_WEIGHT, transcendentals=0),
        name="joined",
    )(low, high)


def ride_sum_kernel(rows, stack_ref, out_ref, rides, sems):
    n_ride = rides.shape[1]
    copies = []
    for i in range(SIDE):
        ride = stack_ref.at[pl.ds(i * (rows + n_ride) + rows, n_ride)]
        copies.append(pltpu.make_async_copy(ride, rides.at[i], sems.at[i]))
        copies[-1].start()
    for copy in copies:
        copy.wait()
    total = rides[0].astype(F32)
    for i in range(1, SIDE):
        total = total + rides[i].astype(F32)
    out_ref[...] = jnp.concatenate(jnp.split(total.astype(BF16), SIDE, axis=1), axis=0)


def ride_sum(stack, rows):
    n_ride, width = stack.shape[0] // SIDE - rows, stack.shape[1]
    return pl.pallas_call(
        functools.partial(ride_sum_kernel, rows),
        out_shape=jax.ShapeDtypeStruct((n_ride * SIDE, width // SIDE), BF16),
        in_specs=[pl.BlockSpec(memory_space=pl.ANY)],
        out_specs=pl.BlockSpec(memory_space=pltpu.VMEM),
        scratch_shapes=[
            pltpu.VMEM((SIDE, n_ride, width), BF16),
            pltpu.SemaphoreType.DMA((SIDE,)),
        ],
        name="ride_sum",
    )(stack)


def give_copies(parts, other, sources, out_ref, sems):
    width = out_ref.shape[1]
    columns = pl.ds(pl.multiple_of(other * width, width), width)
    copies, at = [], 0
    for i, (which, row, n) in enumerate(parts):
        source = sources[which].at[pl.ds(row, n), columns]
        copies.append(pltpu.make_async_copy(source, out_ref.at[pl.ds(at, n)], sems.at[i]))
        copies[-1].start()
        at += n
    return copies


def give_kernel(parts, core_ref, *refs):
    sources, (out_ref, sems) = refs[:-2], refs[-2:]
    for copy in give_copies(parts, 1 - core_ref[0], sources, out_ref, sems):
        copy.wait()


def give_half(core, arrays, rows):
    any_spec = pl.BlockSpec(memory_space=pl.ANY)
    parts = [(i, at, rows) for i, a in enumerate(arrays) for at in range(0, a.shape[0], rows)]
    return pl.pallas_call(
        functools.partial(give_kernel, parts),
        out_shape=jax.ShapeDtypeStruct((len(parts) * rows, arrays[0].shape[1] // 2), BF16),
        in_specs=[pl.BlockSpec(memory_space=pltpu.SMEM)] + [any_spec] * len(arrays),
        out_specs=pl.BlockSpec(memory_space=pltpu.VMEM),
        scratch_shapes=[pltpu.SemaphoreType.DMA((len(parts),))],
        name="give",
    )(core, *arrays)


def give_near_kernel(parts, at_ride, place_ref, quarter_ref, *refs):
    sources, (out_ref, sums_ref, rides, sems) = refs[:-4], refs[-4:]
    copies = give_copies(parts, 1 - place_ref[0], sources, out_ref, sems)
    for k, far in enumerate(sources[-3:]):
        ride = far.at[pl.ds(at_ride, rides.shape[1])]
        copies.append(pltpu.make_async_copy(ride, rides.at[k], sems.at[len(parts) + k]))
        copies[-1].start()
    n = quarter_ref.shape[0]
    sums_ref[pl.ds(pl.multiple_of(place_ref[1] * n, n), n)] = quarter_ref[...]
    for copy in copies:
        copy.wait()
    for k in range(3):
        source = (place_ref[1] + SIDE - 1 - k) % SIDE
        ride = jnp.concatenate(jnp.split(rides[k], SIDE, axis=1), axis=0)
        sums_ref[pl.ds(pl.multiple_of(source * n, n), n)] = ride
    at = sum(part[2] for part in parts)
    out_ref[at:] = jnp.concatenate(jnp.split(sums_ref[...], 2, axis=0), axis=1)


def give_near(place, quarter, arrays, steps, rows):
    width = arrays[0].shape[1]
    at_ride = arrays[-1].shape[0] // rows * rows
    n_ride = arrays[-1].shape[0] - at_ride
    n, columns = quarter.shape
    parts = [
        (i, at, rows)
        for i, (a, step) in enumerate(zip(arrays, steps))
        for at in range(0, a.shape[0] - rows + 1, step)
    ]
    vmem, any_spec = pl.BlockSpec(memory_space=pltpu.VMEM), pl.BlockSpec(memory_space=pl.ANY)
    n_sums = SIDE * n * columns * 2 // width
    return pl.pallas_call(
        functools.partial(give_near_kernel, parts, at_ride),
        out_shape=(
            jax.ShapeDtypeStruct((len(parts) * rows + n_sums, width // 2), BF16),
            jax.ShapeDtypeStruct((SIDE * n, columns), BF16),
        ),
        in_specs=[pl.BlockSpec(memory_space=pltpu.SMEM), vmem] + [any_spec] * len(arrays),
        out_specs=(vmem,) * 2,
        scratch_shapes=[
            pltpu.VMEM((3, n_ride, width), BF16),
            pltpu.SemaphoreType.DMA((len(parts) + 3,)),
        ],
        name="give_near",
    )(place, quarter, *arrays)


def frozen_kernel(n_held, parts, core_ref, order_ref, *refs):
    sources, (mine, other, own, came, sems) = refs[:-5], refs[-5:]
    rows, cols = mine.shape
    width = own.shape[1]
    blocks = own.shape[0] // rows
    columns = pl.ds(pl.multiple_of(core_ref[0] * width, width), width)
    copies, at = [], 0
    for i, (which, row) in enumerate(parts):
        target = (own if i < blocks else came).at[pl.ds(i % blocks * rows, rows)]
        source = sources[which].at[pl.ds(row, rows), columns if which < n_held else pl.ds(0, width)]
        copies.append(pltpu.make_async_copy(source, target, sems.at[i]))
    for copy in copies[blocks:] + copies[:blocks]:
        copy.start()
    for copy in copies[blocks:]:
        copy.wait()

    def matched(i):
        return came[pl.ds(pl.multiple_of(order_ref[i] * rows, rows), rows)]

    def held(i):
        copies[i].wait()
        return own[i * rows : (i + 1) * rows]

    def product(left, right):
        return lax.dot_general(left, right, NT, preferred_element_type=F32)

    @pl.when(core_ref[0] == 0)
    def _():
        total = product(held(0), matched(0))
        for i in range(1, blocks):
            total = total + product(held(i), matched(i))
        mine[...] = total[:, :cols]
        other[...] = total[:, cols:]

    @pl.when(core_ref[0] == 1)
    def _():
        total = product(matched(0), held(0))
        for i in range(1, blocks):
            total = total + product(matched(i), held(i))
        mine[...] = total[:, cols:]
        other[...] = total[:, :cols]


def frozen_product(core, order, own, came, rows):
    arrays = [a for a, _ in (*own, *came)]
    parts = []
    for i, (a, step) in enumerate((*own, *came)):
        parts += [(i, at) for at in range(0, a.shape[0] - rows + 1, step)]
    width = came[0][0].shape[1]
    held = pltpu.VMEM((len(parts) // 2 * rows, width), BF16)
    return pl.pallas_call(
        functools.partial(frozen_kernel, len(own), parts),
        out_shape=(jax.ShapeDtypeStruct((rows, rows // 2), F32),) * 2,
        in_specs=[pl.BlockSpec(memory_space=pltpu.SMEM)] * 2
        + [pl.BlockSpec(memory_space=pl.ANY)] * len(arrays),
        out_specs=(pl.BlockSpec(memory_space=pltpu.VMEM),) * 2,
        scratch_shapes=[held, held, pltpu.SemaphoreType.DMA((len(parts),))],
        compiler_params=pltpu.CompilerParams(vmem_limit_bytes=56 * 1024 * 1024),
        cost_estimate=pl.CostEstimate(
            flops=4 * rows * held.shape[0] * width, bytes_accessed=24 << 20, transcendentals=0
        ),
        name="frozen",
    )(core, order, *arrays)


def block_order(core, dp, tensor):
    stage = jnp.array([0] * 4 + [1, 2] * 4 + [3] * 4, jnp.int32)
    step = jnp.array([0, 1, 2, 3, 0, 0, 1, 1, 2, 2, 3, 3, 0, 1, 2, 3], jnp.int32)
    first = core == 0
    mine, theirs = jnp.where(first, tensor, dp) // SIDE, jnp.where(first, dp, tensor) // SIDE
    high = jnp.where(stage == 0, step, (mine - step) % SIDE)
    shift = jnp.where(stage == 2, 3, jnp.where(stage == 3, 2, stage))
    low = jnp.where(first, (tensor - shift) % SIDE, (dp % SIDE) ^ stage)
    back = (tensor - low) % SIDE
    back = jnp.where(back == 2, 3, jnp.where(back == 3, 2, back))
    stage = jnp.where(first, (dp % SIDE) ^ low, back)
    step = (theirs - high) % SIDE
    return jnp.where(
        stage == 0, high, jnp.where(stage == 3, 12 + step, 3 + stage + 2 * step)
    )


def window(i, rows):
    return max(i - 1, 0) * rows


def forward_kernel(
    scale, place_ref, q_ref, label_ref, lower_ref, keys_ref, values_ref, rows_ref, taps_ref,
    upper_ref, slab_ref, band_ref, out_ref, inner_ref, k_ref, v_ref, give_ref, sems,
):
    head = k_ref.shape[1]
    n, n_taps, (rank, width) = rows_ref.shape[0], taps_ref.shape[0], upper_ref.shape
    at_upper = n + n_taps
    at_inner = at_upper + rank // 2
    mine = pl.ds(pl.multiple_of(place_ref[2] * head, head), head)

    def copy(i, source, target):
        return pltpu.make_async_copy(source, target, sems.at[i])

    seen = [copy(0, keys_ref.at[:, mine], k_ref), copy(1, values_ref.at[:, mine], v_ref)]
    given = [copy(2, taps_ref, give_ref.at[pl.ds(n, n_taps)])]
    for i in range(2):
        target = give_ref.at[pl.ds(at_upper, rank // 2), pl.ds(i * width, width)]
        given.append(copy(3 + i, upper_ref.at[pl.ds(i * (rank // 2), rank // 2)], target))
    for one in seen + given:
        one.start()

    @pl.when(place_ref[0] == 0)
    def _():
        copy(5, slab_ref, give_ref.at[pl.ds(0, n)]).start()

    @pl.when(place_ref[0] == 1)
    def _():
        copy(5, rows_ref, give_ref.at[pl.ds(0, n)]).start()

    for one in seen:
        one.wait()
    rows = band_ref.shape[2] // 2
    labels = label_ref[...].astype(F32)
    ahead = lax.broadcasted_iota(jnp.int32, (rows, 2 * rows), 0)
    ahead = ahead - lax.broadcasted_iota(jnp.int32, (rows, 2 * rows), 1)
    for i in range(q_ref.shape[0] // rows):
        at, low = i * rows, window(i, rows)
        own = jnp.broadcast_to(labels[:, at : at + rows], (rows, rows)).T
        own = jnp.concatenate([own, own], axis=1)
        allowed = (ahead >= low - at) & (own == labels[:, low : low + 2 * rows])
        for h in range(band_ref.shape[0]):
            cols = slice(h * head, (h + 1) * head)
            scores = lax.dot_general(
                q_ref[at : at + rows, cols],
                k_ref[low : low + 2 * rows],
                NT,
                preferred_element_type=F32,
            )
            scores = jnp.where(allowed, scores * scale, -jnp.inf)
            probs = jnp.exp(scores - jnp.max(scores, axis=1, keepdims=True))
            probs = probs / jnp.sum(probs, axis=1, keepdims=True)
            band_ref[h, at : at + rows] = probs
            out_ref[at : at + rows, cols] = jnp.dot(
                probs.astype(BF16), v_ref[low : low + 2 * rows], preferred_element_type=F32
            ).astype(BF16)
    inner = lax.dot_general(out_ref[...], lower_ref[...], NT, preferred_element_type=F32)
    inner_ref[...] = inner
    inner = jnp.split(inner.astype(BF16), 2 * width // rank, axis=0)
    give_ref[at_inner:] = jnp.concatenate(inner, axis=1)
    for one in given:
        one.wait()
    copy(5, rows_ref, give_ref.at[pl.ds(0, n)]).wait()


def forward(place, queries, labels, lower, keys, values, rows, taps, upper, slab):
    n, width = queries.shape
    heads, rank = width // HEAD_WIDTH, lower.shape[0]
    any_spec = pl.BlockSpec(memory_space=pl.ANY)
    vmem = pl.BlockSpec(memory_space=pltpu.VMEM)
    n_give = rows.shape[0] + taps.shape[0] + rank // 2 + n * rank // rows.shape[1]
    return pl.pallas_call(
        functools.partial(forward_kernel, HEAD_WIDTH**-0.5),
        out_shape=(
            jax.ShapeDtypeStruct((heads, n, 2 * SEGMENT_MOST), F32),
            jax.ShapeDtypeStruct((n, width), BF16),
            jax.ShapeDtypeStruct((n, rank), F32),
            jax.ShapeDtypeStruct((n, HEAD_WIDTH), BF16),
            jax.ShapeDtypeStruct((n, HEAD_WIDTH), BF16),
            jax.ShapeDtypeStruct((n_give, rows.shape[1]), BF16),
        ),
        in_specs=[pl.BlockSpec(memory_space=pltpu.SMEM)] + [vmem] * 3 + [any_spec] * 6,
        out_specs=(vmem,) * 6,
        scratch_shapes=[pltpu.SemaphoreType.DMA((6,))],
        name="attention",
    )(place, queries, labels, lower, keys, values, rows, taps, upper, slab)


def backward_kernel(
    scale, core_ref, mine_ref, came_ref, adapter_ref, lower_ref, band_ref, out_ref, q_ref, k_ref,
    v_ref, query_ref, keep_ref, give_ref, key_sum, value_sum,
):
    rows = band_ref.shape[2] // 2
    head = k_ref.shape[1]
    key_sum[...] = jnp.zeros_like(key_sum)
    value_sum[...] = jnp.zeros_like(value_sum)
    for i in range(q_ref.shape[0] // rows):
        at, low = i * rows, window(i, rows)
        part, seen = slice(at, at + rows), slice(low, low + 2 * rows)
        adapter = adapter_ref[part, lower_ref.shape[0] :]
        lora = jnp.dot(adapter, lower_ref[...], preferred_element_type=F32)
        gradient = (mine_ref[part] + came_ref[part] + adapter_scale * lora).astype(BF16)
        for h in range(band_ref.shape[0]):
            cols = slice(h * head, (h + 1) * head)
            own = gradient[:, cols]
            probs = band_ref[h, part]
            terms = jnp.sum(
                own.astype(F32) * out_ref[part, cols].astype(F32), axis=1, keepdims=True
            )
            prob_grad = lax.dot_general(own, v_ref[seen], NT, preferred_element_type=F32)
            score_grad = (probs * (prob_grad - terms)).astype(BF16)
            query_grad = jnp.dot(score_grad, k_ref[seen], preferred_element_type=F32)
            query_ref[part, cols] = (scale * query_grad).astype(BF16)
            key_sum[seen] += lax.dot_general(
                score_grad, q_ref[part, cols], TN, preferred_element_type=F32
            )
            value_sum[seen] += lax.dot_general(
                probs.astype(BF16), own, TN, preferred_element_type=F32
            )
    quarter = head // 4
    for source, factor, at in ((key_sum, scale, 0), (value_sum, None, 2 * quarter)):
        total = source[...] if factor is None else source[...] * factor
        even = jnp.concatenate([total[:, :quarter], total[:, 2 * quarter : 3 * quarter]], axis=1)
        odd = jnp.concatenate([total[:, quarter : 2 * quarter], total[:, 3 * quarter :]], axis=1)
        first = core_ref[0] == 0
        keep_ref[:, at : at + 2 * quarter] = jnp.where(first, even, odd)
        give_ref[:, at : at + 2 * quarter] = jnp.where(first, odd, even)


def backward(core, mine, came, adapter, lower, band, out, queries, key_head, value_head):
    n, width = queries.shape
    half = jax.ShapeDtypeStruct((n, HEAD_WIDTH), F32)
    return pl.pallas_call(
        functools.partial(backward_kernel, HEAD_WIDTH**-0.5),
        out_shape=(jax.ShapeDtypeStruct((n, width), BF16), half, half),
        in_specs=[pl.BlockSpec(memory_space=pltpu.SMEM)]
        + [pl.BlockSpec(memory_space=pltpu.VMEM)] * 9,
        out_specs=(pl.BlockSpec(memory_space=pltpu.VMEM),) * 3,
        scratch_shapes=[pltpu.VMEM((n, HEAD_WIDTH), F32)] * 2,
        cost_estimate=pl.CostEstimate(
            flops=20 * n * width * 2 * SEGMENT_MOST, bytes_accessed=16 << 20, transcendentals=0
        ),
        name="attention_gradient",
    )(core, mine, came, adapter, lower, band, out, queries, key_head, value_head)


def quarters_kernel(chip_ref, keep_ref, came_ref, out_ref, give_ref):
    total = keep_ref[...] + came_ref[...]
    n, quarter = total.shape[0] // 2, total.shape[1] // 4
    even = jnp.concatenate([total[:, :quarter], total[:, 2 * quarter : 3 * quarter]], axis=1)
    odd = jnp.concatenate([total[:, quarter : 2 * quarter], total[:, 3 * quarter :]], axis=1)
    first = chip_ref[0] == 0
    out_ref[...] = jnp.where(first, even, odd)
    give = jnp.where(first, odd, even).astype(BF16)
    give_ref[...] = jnp.concatenate([give[:n], give[n:]], axis=1)


def quarters_kept(chip, keep, came):
    n, width = keep.shape
    return pl.pallas_call(
        quarters_kernel,
        out_shape=(
            jax.ShapeDtypeStruct((n, width // 2), F32),
            jax.ShapeDtypeStruct((n // 2, width), BF16),
        ),
        in_specs=[pl.BlockSpec(memory_space=pltpu.SMEM)]
        + [pl.BlockSpec(memory_space=pltpu.VMEM)] * 2,
        out_specs=(pl.BlockSpec(memory_space=pltpu.VMEM),) * 2,
        name="quarters",
    )(chip, keep, came)


def rounded_sum_kernel(keep_ref, came_ref, key_ref, value_ref):
    came = came_ref[...].astype(F32)
    quarter = key_ref.shape[0]
    came = jnp.concatenate([came[:, : 2 * quarter], came[:, 2 * quarter :]], axis=0)
    total = (keep_ref[...] + came).T.astype(BF16)
    key_ref[...] = total[:quarter]
    value_ref[...] = total[quarter:]


def rounded_sum(keep, came):
    n, width = keep.shape
    vmem = pl.BlockSpec(memory_space=pltpu.VMEM)
    return pl.pallas_call(
        rounded_sum_kernel,
        out_shape=(jax.ShapeDtypeStruct((width // 2, n), BF16),) * 2,
        in_specs=[vmem] * 2,
        out_specs=(vmem,) * 2,
        name="rounded_sum",
    )(keep, came)


def on_device(
    rotated_queries,
    rotated_keys,
    stored_values,
    segment_labels,
    output_gradient,
    draft_loss_gradients,
    tapped_row_index,
    output_projector,
    lower_factor_weight,
    upper_factor_weight,
):
    seq_len = rotated_queries.shape[1]
    head_size = HEAD_WIDTH
    heads_dev = rotated_queries.shape[2] // head_size
    group_size = QUERY_HEAD_COUNT // KVH
    score_scale = head_size ** (-0.5)
    core = lax.axis_index("draft")
    tensor = lax.axis_index("tensor")
    dp = lax.axis_index("dp")
    upper_core = core == 1
    rank_index = tensor * 2 + core
    kv_head = rank_index * heads_dev // group_size
    width = output_projector.shape[1] // 2
    rank = lower_factor_weight.shape[1]

    core_ref = core.reshape(1)
    y = tensor // SIDE
    place = jnp.stack([core, y, kv_head]).astype(jnp.int32)
    rows, taps = output_gradient[0], draft_loss_gradients[0]
    queries, lower = rotated_queries[0], lower_factor_weight.T
    band, output_flattened, inner_piece, key_head, value_head, give = forward(
        place,
        queries,
        segment_labels,
        lower,
        rotated_keys[0],
        stored_values[0],
        rows,
        taps,
        upper_factor_weight,
        output_projector,
    )
    block, _, stacked = blend(
        place,
        tapped_row_index,
        rows,
        taps,
        upper_factor_weight,
        output_projector,
        swapped(give, "draft", 1),
        inner_piece,
    )
    z1, z2 = near_move(block, 1, 1), near_move(block, 3, 2)

    half = seq_len // 2
    own_far = spread(stacked, AXES, far_groups())
    quarter = ride_sum(own_far, seq_len)
    from_z = [first_swapped(quarter, mask).astype(F32) for mask in (1, 2, 3)]
    quarter = ((quarter.astype(F32) + from_z[1]) + (from_z[0] + from_z[2])).astype(BF16)
    low = near_move(jnp.where(upper_core, block[:half], z1[:half]), 1, 3)
    high = near_move(jnp.where(upper_core, block[half:], z2[half:]), 3, 3)
    last = joined(low, high)
    near = jnp.concatenate([z1, z2, widened(quarter, SIDE)], axis=0)
    near_far = [far_move(near, k) for k in (1, 2, 3)]
    give, sums = give_near(
        place,
        after(quarter, last),
        [own_far, z1, z2, *near_far],
        [own_far.shape[0] // SIDE] + [seq_len] * 5,
        seq_len,
    )
    came_near = swapped(give, "draft", 1)
    residual = lax.dynamic_slice_in_dim(came_near, y * seq_len, seq_len, 0)
    residual = jnp.where(upper_core, residual, block[:, :width])
    last_far = [far_move(last, k) for k in (1, 2, 3)]
    sums = jnp.where(upper_core, narrowed(came_near[12 * seq_len :], 2), sums)
    adapter_inner, adapter_gradient = sums[:, :rank], sums[:, rank:]

    lower_piece = lax.dot_general(adapter_gradient, output_flattened, TN, preferred_element_type=F32)
    upper_piece = lax.dot_general(adapter_inner, residual, TN, preferred_element_type=F32)
    factor = jnp.concatenate([lower_piece, upper_piece], axis=0)
    factor = factor + swapped(factor, "dp", 1)
    from_dp = swapped(factor, "dp", 2)
    give = give_half(core_ref, [after(last, came_near, factor), *last_far], seq_len)
    came_last = swapped(give, "draft", 1)

    part_mine, part_other = frozen_product(
        core_ref,
        block_order(core, dp, tensor),
        [(own_far, own_far.shape[0] // SIDE)]
        + [(a, seq_len) for a in (z1, z2, *near_far, last, *last_far)],
        [(came_near, seq_len), (came_last, seq_len)],
        seq_len,
    )
    factor = factor + after(from_dp, part_mine)
    came = swapped(after(part_other, factor), "draft", 1)
    from_dp = swapped(factor, "dp", 4)
    query_grad, keep, give = backward(
        core_ref,
        part_mine,
        came,
        sums,
        lower,
        band,
        output_flattened,
        queries,
        key_head,
        value_head,
    )
    factor = factor + after(from_dp, give)
    came = swapped(after(give, factor), "draft", 1)
    from_dp = swapped(factor, "dp", 8)
    keep, give = quarters_kept((tensor & 1).reshape(1), keep, came)
    came = swapped(give, "tensor", 1)
    factor = factor + after(from_dp, give)
    factor = factor * (adapter_scale / lax.axis_size("dp"))
    lower_gradient, upper_gradient = factor[:rank].T, factor[rank:]
    key_grad, value_grad = rounded_sum(keep, came)
    key_grad, value_grad = key_grad.T[None], value_grad.T[None]
    query_grad = query_grad[None]
    return (query_grad, key_grad, value_grad, lower_gradient, upper_gradient)


def solution(mesh):
    in_specs = (
        P("dp", None, ("tensor", "draft")),
        P("dp", None, None),
        P("dp", None, None),
        P("dp", None),
        P("dp", "draft", "tensor"),
        P("dp", "draft", "tensor"),
        P("dp", None),
        P(("tensor", "draft"), "dp"),
        P(("tensor", "draft"), None),
        P(None, ("tensor", "draft")),
    )
    out_specs = (
        P("dp", None, ("tensor", "draft")),
        P("dp", None, ("tensor", "draft")),
        P("dp", None, ("tensor", "draft")),
        P(("tensor", "draft"), None),
        P(None, ("tensor", "draft")),
    )
    return jax.shard_map(
        on_device, mesh=mesh, in_specs=in_specs, out_specs=out_specs, check_vma=False
    )
```

```python
import functools

import jax
import jax.numpy as jnp
from jax import lax
from jax.experimental import pallas as pl
from jax.experimental.pallas import tpu as pltpu
from jax.sharding import PartitionSpec as P

QUERY_HEAD_COUNT = 64
KVH = 8
HEAD_WIDTH = 128
SIDE = 4
SEGMENT_MOST = 128

adapter_scale = 2.0

F32, BF16 = jnp.float32, jnp.bfloat16
NT = (((1,), (1,)), ((), ()))
TN = (((0,), (0,)), ((), ()))


AXES = ("dp", "tensor", "draft")


def moved(array, residual_to, slab_to):
    n_dp, n_tensor = lax.axis_size("dp"), lax.axis_size("tensor")
    pairs = []
    for d in range(n_dp):
        for t in range(n_tensor):
            at = (d * n_tensor + t) * 2
            pairs.append((at, (d * n_tensor + residual_to(t)) * 2))
            pairs.append((at + 1, (slab_to(d) * n_tensor + t) * 2 + 1))
    return lax.ppermute(array, AXES, pairs)


def spread(stacked, axes, groups):
    return lax.all_to_all(stacked, axes, 0, 0, axis_index_groups=groups, tiled=True)


def high_groups():
    return [[i * SIDE + j for i in range(SIDE)] for j in range(SIDE)]


def far_groups():
    n_dp, n_tensor = lax.axis_size("dp"), lax.axis_size("tensor")
    groups = []
    for one in high_groups():
        groups += [[(d * n_tensor + t) * 2 for t in one] for d in range(n_dp)]
        groups += [[(d * n_tensor + t) * 2 + 1 for d in one] for t in range(n_tensor)]
    return groups


def far_move(array, k):
    step = lambda i: (i + k * SIDE) % (SIDE * SIDE)
    return moved(array, step, step)


def near_move(array, shift, mask):
    ahead = lambda t: t // SIDE * SIDE + (t + shift) % SIDE
    return moved(array, ahead, lambda d: d ^ mask)


def first_swapped(array, mask):
    n = lax.axis_size("dp") * lax.axis_size("tensor")
    return lax.ppermute(array, AXES, [(2 * i, 2 * (i ^ mask)) for i in range(n)])


def swapped(array, axis, mask):
    return lax.ppermute(array, axis, [(i, i ^ mask) for i in range(lax.axis_size(axis))])


def after(array, *earlier):
    return lax.optimization_barrier((array, *earlier))[0]


def blend_kernel(
    place_ref, tapped_ref, rows_ref, taps_ref, upper_ref, slab_ref, came_ref, inner_ref,
    block_ref, sums_ref, stack_ref,
):
    n, n_taps, rank = rows_ref.shape[0], taps_ref.shape[0], upper_ref.shape[0]
    width = upper_ref.shape[1]
    at_upper = n + n_taps
    at_inner = at_upper + rank // 2

    @pl.when(place_ref[0] == 0)
    def _():
        taps = jnp.concatenate([taps_ref[...], came_ref[n:at_upper]], axis=0)
        place = lax.broadcasted_iota(jnp.int32, (2 * n, 2 * n_taps), 0)
        hit = jnp.where(place == tapped_ref[...], 1.0, 0.0).astype(BF16)
        spread = jnp.dot(hit, taps, preferred_element_type=F32)
        block_ref[:n] = (rows_ref[...].astype(F32) + spread[:n]).astype(BF16)
        block_ref[n:] = (came_ref[:n].astype(F32) + spread[n:]).astype(BF16)
        upper = came_ref[at_upper:at_inner]
        upper = jnp.concatenate([upper[:, :width], upper[:, width:]], axis=0)
        lora = lax.dot_general(
            block_ref[:, :width], upper_ref[...], NT, preferred_element_type=F32
        ) + lax.dot_general(block_ref[:, width:], upper, NT, preferred_element_type=F32)
        inner = came_ref[at_inner:].astype(F32)
        inner = [inner[:, i * rank : (i + 1) * rank] for i in range(inner.shape[1] // rank)]
        inner = inner_ref[...] + jnp.concatenate(inner, axis=0)
        sums_ref[...] = jnp.concatenate([inner, lora], axis=1)

    @pl.when(place_ref[0] == 1)
    def _():
        block_ref[:n] = came_ref[:n]
        block_ref[n:] = slab_ref[...]
        sums_ref[...] = jnp.zeros_like(sums_ref)

    quarter = 2 * n // SIDE
    step = stack_ref.shape[0] // SIDE
    for i in range(SIDE):
        at = i * step
        stack_ref[at : at + 2 * n] = block_ref[...]
        share = sums_ref[i * quarter : (i + 1) * quarter].astype(BF16)
        stack_ref[at + 2 * n : at + step] = jnp.concatenate(
            jnp.split(share, SIDE, axis=0), axis=1
        )


def blend(place, tapped, rows, taps, upper, slab, came, inner):
    n, width = rows.shape
    ride = 2 * n // SIDE * 2 * upper.shape[0] // width
    vmem = pl.BlockSpec(memory_space=pltpu.VMEM)
    return pl.pallas_call(
        blend_kernel,
        out_shape=(
            jax.ShapeDtypeStruct((2 * n, width), BF16),
            jax.ShapeDtypeStruct((2 * n, 2 * upper.shape[0]), F32),
            jax.ShapeDtypeStruct((SIDE * (2 * n + ride), width), BF16),
        ),
        in_specs=[pl.BlockSpec(memory_space=pltpu.SMEM)] + [vmem] * 7,
        out_specs=(vmem,) * 3,
        name="blend",
    )(place, tapped, rows, taps, upper, slab, came, inner)


def widened(array, n):
    return jnp.concatenate(jnp.split(array, n, axis=0), axis=1)


def narrowed(array, n):
    return jnp.concatenate(jnp.split(array, n, axis=1), axis=0)


def ride_sum_kernel(rows, stack_ref, out_ref, rides, sems):
    n_ride = rides.shape[1]
    copies = []
    for i in range(SIDE):
        ride = stack_ref.at[pl.ds(i * (rows + n_ride) + rows, n_ride)]
        copies.append(pltpu.make_async_copy(ride, rides.at[i], sems.at[i]))
        copies[-1].start()
    for copy in copies:
        copy.wait()
    total = rides[0].astype(F32)
    for i in range(1, SIDE):
        total = total + rides[i].astype(F32)
    out_ref[...] = jnp.concatenate(jnp.split(total.astype(BF16), SIDE, axis=1), axis=0)


def ride_sum(stack, rows):
    n_ride, width = stack.shape[0] // SIDE - rows, stack.shape[1]
    return pl.pallas_call(
        functools.partial(ride_sum_kernel, rows),
        out_shape=jax.ShapeDtypeStruct((n_ride * SIDE, width // SIDE), BF16),
        in_specs=[pl.BlockSpec(memory_space=pl.ANY)],
        out_specs=pl.BlockSpec(memory_space=pltpu.VMEM),
        scratch_shapes=[
            pltpu.VMEM((SIDE, n_ride, width), BF16),
            pltpu.SemaphoreType.DMA((SIDE,)),
        ],
        name="ride_sum",
    )(stack)


def give_copies(parts, other, sources, out_ref, sems):
    width = out_ref.shape[1]
    columns = pl.ds(pl.multiple_of(other * width, width), width)
    copies, at = [], 0
    for i, (which, row, n) in enumerate(parts):
        source = sources[which].at[pl.ds(row, n), columns]
        copies.append(pltpu.make_async_copy(source, out_ref.at[pl.ds(at, n)], sems.at[i]))
        copies[-1].start()
        at += n
    return copies


def give_kernel(parts, core_ref, *refs):
    sources, (out_ref, sems) = refs[:-2], refs[-2:]
    for copy in give_copies(parts, 1 - core_ref[0], sources, out_ref, sems):
        copy.wait()


def give_half(core, arrays, rows):
    any_spec = pl.BlockSpec(memory_space=pl.ANY)
    parts = [(i, at, rows) for i, a in enumerate(arrays) for at in range(0, a.shape[0], rows)]
    return pl.pallas_call(
        functools.partial(give_kernel, parts),
        out_shape=jax.ShapeDtypeStruct((len(parts) * rows, arrays[0].shape[1] // 2), BF16),
        in_specs=[pl.BlockSpec(memory_space=pltpu.SMEM)] + [any_spec] * len(arrays),
        out_specs=pl.BlockSpec(memory_space=pltpu.VMEM),
        scratch_shapes=[pltpu.SemaphoreType.DMA((len(parts),))],
        name="give",
    )(core, *arrays)


def give_near_kernel(parts, at_ride, place_ref, quarter_ref, *refs):
    sources, (out_ref, sums_ref, rides, sems) = refs[:-4], refs[-4:]
    copies = give_copies(parts, 1 - place_ref[0], sources, out_ref, sems)
    for k, far in enumerate(sources[-3:]):
        ride = far.at[pl.ds(at_ride, rides.shape[1])]
        copies.append(pltpu.make_async_copy(ride, rides.at[k], sems.at[len(parts) + k]))
        copies[-1].start()
    n = quarter_ref.shape[0]
    sums_ref[pl.ds(pl.multiple_of(place_ref[1] * n, n), n)] = quarter_ref[...]
    for copy in copies:
        copy.wait()
    for k in range(3):
        source = (place_ref[1] + SIDE - 1 - k) % SIDE
        ride = jnp.concatenate(jnp.split(rides[k], SIDE, axis=1), axis=0)
        sums_ref[pl.ds(pl.multiple_of(source * n, n), n)] = ride
    at = sum(part[2] for part in parts)
    out_ref[at:] = jnp.concatenate(jnp.split(sums_ref[...], 2, axis=0), axis=1)


def give_near(place, quarter, arrays, steps, rows):
    width = arrays[0].shape[1]
    at_ride = arrays[-1].shape[0] // rows * rows
    n_ride = arrays[-1].shape[0] - at_ride
    n, columns = quarter.shape
    parts = [
        (i, at, rows)
        for i, (a, step) in enumerate(zip(arrays, steps))
        for at in range(0, a.shape[0] - rows + 1, step)
    ]
    vmem, any_spec = pl.BlockSpec(memory_space=pltpu.VMEM), pl.BlockSpec(memory_space=pl.ANY)
    n_sums = SIDE * n * columns * 2 // width
    return pl.pallas_call(
        functools.partial(give_near_kernel, parts, at_ride),
        out_shape=(
            jax.ShapeDtypeStruct((len(parts) * rows + n_sums, width // 2), BF16),
            jax.ShapeDtypeStruct((SIDE * n, columns), BF16),
        ),
        in_specs=[pl.BlockSpec(memory_space=pltpu.SMEM), vmem] + [any_spec] * len(arrays),
        out_specs=(vmem,) * 2,
        scratch_shapes=[
            pltpu.VMEM((3, n_ride, width), BF16),
            pltpu.SemaphoreType.DMA((len(parts) + 3,)),
        ],
        name="give_near",
    )(place, quarter, *arrays)


def frozen_kernel(n_held, parts, core_ref, place_ref, *refs):
    sources, (mine, other, own, came, sems) = refs[:-5], refs[-5:]
    rows, cols = mine.shape
    blocks = len(parts) // 2
    width = own.shape[1] // blocks
    columns = pl.ds(pl.multiple_of(core_ref[0] * width, width), width)
    copies = []
    for i, (which, row) in enumerate(parts):
        if i < blocks:
            target = own.at[:, pl.ds(i * width, width)]
        else:
            at = pl.multiple_of(place_ref[i - blocks] * width, width)
            target = came.at[:, pl.ds(at, width)]
        source = sources[which].at[pl.ds(row, rows), columns if which < n_held else pl.ds(0, width)]
        copies.append(pltpu.make_async_copy(source, target, sems.at[i]))
    for copy in copies[blocks:] + copies[:blocks]:
        copy.start()
    for copy in copies[blocks:]:
        copy.wait()
    together = blocks // 4

    def total(first, second):
        result = None
        for i in range(0, blocks, together):
            for copy in copies[i : i + together]:
                copy.wait()
            depth = slice(i * width, (i + together) * width)
            term = lax.dot_general(
                first[:, depth], second[:, depth], NT, preferred_element_type=F32
            )
            result = term if result is None else result + term
        return result

    @pl.when(core_ref[0] == 0)
    def _():
        product = total(own, came)
        mine[...] = product[:, :cols]
        other[...] = product[:, cols:]

    @pl.when(core_ref[0] == 1)
    def _():
        product = total(came, own)
        mine[...] = product[:, cols:]
        other[...] = product[:, :cols]


def frozen_product(core, place, own, came, rows):
    arrays = [a for a, _ in (*own, *came)]
    parts = []
    for i, (a, step) in enumerate((*own, *came)):
        parts += [(i, at) for at in range(0, a.shape[0] - rows + 1, step)]
    width = came[0][0].shape[1]
    held = pltpu.VMEM((rows, len(parts) // 2 * width), BF16)
    return pl.pallas_call(
        functools.partial(frozen_kernel, len(own), parts),
        out_shape=(jax.ShapeDtypeStruct((rows, rows // 2), F32),) * 2,
        in_specs=[pl.BlockSpec(memory_space=pltpu.SMEM)] * 2
        + [pl.BlockSpec(memory_space=pl.ANY)] * len(arrays),
        out_specs=(pl.BlockSpec(memory_space=pltpu.VMEM),) * 2,
        scratch_shapes=[held, held, pltpu.SemaphoreType.DMA((len(parts),))],
        compiler_params=pltpu.CompilerParams(vmem_limit_bytes=56 * 1024 * 1024),
        cost_estimate=pl.CostEstimate(
            flops=4 * rows * rows * held.shape[1], bytes_accessed=24 << 20, transcendentals=0
        ),
        name="frozen",
    )(core, place, *arrays)


def block_order(core, dp, tensor):
    stage = jnp.array([0] * 4 + [1, 2] * 4 + [3] * 4, jnp.int32)
    step = jnp.array([0, 1, 2, 3, 0, 0, 1, 1, 2, 2, 3, 3, 0, 1, 2, 3], jnp.int32)
    first = core == 0
    mine, theirs = jnp.where(first, tensor, dp) // SIDE, jnp.where(first, dp, tensor) // SIDE
    high = jnp.where(stage == 0, step, (mine - step) % SIDE)
    shift = jnp.where(stage == 2, 3, jnp.where(stage == 3, 2, stage))
    low = jnp.where(first, (tensor - shift) % SIDE, (dp % SIDE) ^ stage)
    back = (tensor - low) % SIDE
    back = jnp.where(back == 2, 3, jnp.where(back == 3, 2, back))
    stage = jnp.where(first, (dp % SIDE) ^ low, back)
    step = (theirs - high) % SIDE
    return jnp.where(
        stage == 0, high, jnp.where(stage == 3, 12 + step, 3 + stage + 2 * step)
    )


def window(i, rows):
    return max(i - 1, 0) * rows


def forward_kernel(
    scale, place_ref, q_ref, label_ref, lower_ref, keys_ref, values_ref, rows_ref, taps_ref,
    upper_ref, slab_ref, band_ref, out_ref, inner_ref, k_ref, v_ref, give_ref, sems,
):
    head = k_ref.shape[1]
    n, n_taps, (rank, width) = rows_ref.shape[0], taps_ref.shape[0], upper_ref.shape
    at_upper = n + n_taps
    at_inner = at_upper + rank // 2
    mine = pl.ds(pl.multiple_of(place_ref[2] * head, head), head)

    def copy(i, source, target):
        return pltpu.make_async_copy(source, target, sems.at[i])

    seen = [copy(0, keys_ref.at[:, mine], k_ref), copy(1, values_ref.at[:, mine], v_ref)]
    given = [copy(2, taps_ref, give_ref.at[pl.ds(n, n_taps)])]
    for i in range(2):
        target = give_ref.at[pl.ds(at_upper, rank // 2), pl.ds(i * width, width)]
        given.append(copy(3 + i, upper_ref.at[pl.ds(i * (rank // 2), rank // 2)], target))
    for one in seen + given:
        one.start()

    @pl.when(place_ref[0] == 0)
    def _():
        copy(5, slab_ref, give_ref.at[pl.ds(0, n)]).start()

    @pl.when(place_ref[0] == 1)
    def _():
        copy(5, rows_ref, give_ref.at[pl.ds(0, n)]).start()

    for one in seen:
        one.wait()
    rows = band_ref.shape[2] // 2
    labels = label_ref[...].astype(F32)
    ahead = lax.broadcasted_iota(jnp.int32, (rows, 2 * rows), 0)
    ahead = ahead - lax.broadcasted_iota(jnp.int32, (rows, 2 * rows), 1)
    tiles = [(i, h) for i in range(q_ref.shape[0] // rows) for h in range(band_ref.shape[0])]
    scores = {}
    for i, h in tiles:
        at, low = i * rows, window(i, rows)
        scores[i, h] = lax.dot_general(
            q_ref[at : at + rows, h * head : (h + 1) * head],
            k_ref[low : low + 2 * rows],
            NT,
            preferred_element_type=F32,
        )
    allowed = {}
    for i in range(q_ref.shape[0] // rows):
        at, low = i * rows, window(i, rows)
        own = jnp.broadcast_to(labels[:, at : at + rows], (rows, rows)).T
        own = jnp.concatenate([own, own], axis=1)
        allowed[i] = (ahead >= low - at) & (own == labels[:, low : low + 2 * rows])
    probs = {}
    for i, h in tiles:
        masked = jnp.where(allowed[i], scores[i, h] * scale, -jnp.inf)
        raised = jnp.exp(masked - jnp.max(masked, axis=1, keepdims=True))
        probs[i, h] = raised / jnp.sum(raised, axis=1, keepdims=True)
    outs = {}
    for i, h in tiles:
        low = window(i, rows)
        outs[i, h] = jnp.dot(
            probs[i, h].astype(BF16), v_ref[low : low + 2 * rows], preferred_element_type=F32
        ).astype(BF16)
    for i, h in tiles:
        at = i * rows
        band_ref[h, at : at + rows] = probs[i, h]
        out_ref[at : at + rows, h * head : (h + 1) * head] = outs[i, h]
    inner = lax.dot_general(out_ref[...], lower_ref[...], NT, preferred_element_type=F32)
    inner_ref[...] = inner
    inner = jnp.split(inner.astype(BF16), 2 * width // rank, axis=0)
    give_ref[at_inner:] = jnp.concatenate(inner, axis=1)
    for one in given:
        one.wait()
    copy(5, rows_ref, give_ref.at[pl.ds(0, n)]).wait()


def forward(place, queries, labels, lower, keys, values, rows, taps, upper, slab):
    n, width = queries.shape
    heads, rank = width // HEAD_WIDTH, lower.shape[0]
    any_spec = pl.BlockSpec(memory_space=pl.ANY)
    vmem = pl.BlockSpec(memory_space=pltpu.VMEM)
    n_give = rows.shape[0] + taps.shape[0] + rank // 2 + n * rank // rows.shape[1]
    return pl.pallas_call(
        functools.partial(forward_kernel, HEAD_WIDTH**-0.5),
        out_shape=(
            jax.ShapeDtypeStruct((heads, n, 2 * SEGMENT_MOST), F32),
            jax.ShapeDtypeStruct((n, width), BF16),
            jax.ShapeDtypeStruct((n, rank), F32),
            jax.ShapeDtypeStruct((n, HEAD_WIDTH), BF16),
            jax.ShapeDtypeStruct((n, HEAD_WIDTH), BF16),
            jax.ShapeDtypeStruct((n_give, rows.shape[1]), BF16),
        ),
        in_specs=[pl.BlockSpec(memory_space=pltpu.SMEM)] + [vmem] * 3 + [any_spec] * 6,
        out_specs=(vmem,) * 6,
        scratch_shapes=[pltpu.SemaphoreType.DMA((6,))],
        name="attention",
    )(place, queries, labels, lower, keys, values, rows, taps, upper, slab)


def backward_kernel(
    scale, core_ref, mine_ref, came_ref, adapter_ref, lower_ref, band_ref, out_ref, q_ref, k_ref,
    v_ref, query_ref, keep_ref, give_ref, key_sum, value_sum,
):
    rows = band_ref.shape[2] // 2
    head = k_ref.shape[1]
    n = q_ref.shape[0] // rows
    tiles = [(i, h) for i in range(n) for h in range(band_ref.shape[0])]

    def part(i):
        return slice(i * rows, (i + 1) * rows)

    def seen(i):
        return slice(window(i, rows), window(i, rows) + 2 * rows)

    def cols(h):
        return slice(h * head, (h + 1) * head)

    adapter = adapter_ref[:, lower_ref.shape[0] :]
    lora = jnp.dot(adapter, lower_ref[...], preferred_element_type=F32)
    gradient = (mine_ref[...] + came_ref[...] + adapter_scale * lora).astype(BF16)
    own = {(i, h): gradient[part(i), cols(h)] for i, h in tiles}
    prob_grad, terms, score_grad = {}, {}, {}
    for i, h in tiles:
        prob_grad[i, h] = lax.dot_general(
            own[i, h], v_ref[seen(i)], NT, preferred_element_type=F32
        )
    for i, h in tiles:
        product = own[i, h].astype(F32) * out_ref[part(i), cols(h)].astype(F32)
        terms[i, h] = jnp.sum(product, axis=1, keepdims=True)
    probs = {(i, h): band_ref[h, part(i)] for i, h in tiles}
    for i, h in tiles:
        score_grad[i, h] = (probs[i, h] * (prob_grad[i, h] - terms[i, h])).astype(BF16)
    for i, h in tiles:
        query_grad = jnp.dot(score_grad[i, h], k_ref[seen(i)], preferred_element_type=F32)
        query_ref[part(i), cols(h)] = (scale * query_grad).astype(BF16)
    for j in range(n):
        sees = [(j, 0 if j == 0 else 1)] + [(i, 0) for i in (j + 1,) if i < n]
        key_total, value_total = None, None
        for i, side in sees:
            for h in range(band_ref.shape[0]):
                key_part = lax.dot_general(
                    q_ref[part(i), cols(h)], score_grad[i, h][:, part(side)], TN,
                    preferred_element_type=F32,
                )
                value_part = lax.dot_general(
                    own[i, h], probs[i, h][:, part(side)].astype(BF16), TN,
                    preferred_element_type=F32,
                )
                key_total = key_part if key_total is None else key_total + key_part
                value_total = value_part if value_total is None else value_total + value_part
        key_sum[:, part(j)] = key_total
        value_sum[:, part(j)] = value_total
    quarter = head // 4
    first = core_ref[0] == 0
    for source, factor, at in ((key_sum, scale, 0), (value_sum, None, 2 * quarter)):
        total = source[...] if factor is None else source[...] * factor
        for i in (0, 1):
            even = total[2 * i * quarter : (2 * i + 1) * quarter]
            odd = total[(2 * i + 1) * quarter : (2 * i + 2) * quarter]
            rows = slice(at + i * quarter, at + (i + 1) * quarter)
            keep_ref[rows] = jnp.where(first, even, odd)
            give_ref[rows] = jnp.where(first, odd, even)


def backward(core, mine, came, adapter, lower, band, out, queries, key_head, value_head):
    n, width = queries.shape
    half = jax.ShapeDtypeStruct((HEAD_WIDTH, n), F32)
    return pl.pallas_call(
        functools.partial(backward_kernel, HEAD_WIDTH**-0.5),
        out_shape=(jax.ShapeDtypeStruct((n, width), BF16), half, half),
        in_specs=[pl.BlockSpec(memory_space=pltpu.SMEM)]
        + [pl.BlockSpec(memory_space=pltpu.VMEM)] * 9,
        out_specs=(pl.BlockSpec(memory_space=pltpu.VMEM),) * 3,
        scratch_shapes=[pltpu.VMEM((HEAD_WIDTH, n), F32)] * 2,
        cost_estimate=pl.CostEstimate(
            flops=20 * n * width * 2 * SEGMENT_MOST, bytes_accessed=16 << 20, transcendentals=0
        ),
        name="attention_gradient",
    )(core, mine, came, adapter, lower, band, out, queries, key_head, value_head)


def quarters_kernel(chip_ref, keep_ref, came_ref, out_ref, give_ref):
    quarter = keep_ref.shape[0] // 4
    first = chip_ref[0] == 0
    for i in (0, 1):
        at = 2 * i * quarter
        even = keep_ref[at : at + quarter] + came_ref[at : at + quarter]
        odd = keep_ref[at + quarter : at + 2 * quarter] + came_ref[at + quarter : at + 2 * quarter]
        rows = slice(i * quarter, (i + 1) * quarter)
        out_ref[rows] = jnp.where(first, even, odd)
        give_ref[rows] = jnp.where(first, odd, even).astype(BF16)


def quarters_kept(chip, keep, came):
    n, width = keep.shape
    return pl.pallas_call(
        quarters_kernel,
        out_shape=(
            jax.ShapeDtypeStruct((n // 2, width), F32),
            jax.ShapeDtypeStruct((n // 2, width), BF16),
        ),
        in_specs=[pl.BlockSpec(memory_space=pltpu.SMEM)]
        + [pl.BlockSpec(memory_space=pltpu.VMEM)] * 2,
        out_specs=(pl.BlockSpec(memory_space=pltpu.VMEM),) * 2,
        name="quarters",
    )(chip, keep, came)


def on_device(
    rotated_queries,
    rotated_keys,
    stored_values,
    segment_labels,
    output_gradient,
    draft_loss_gradients,
    tapped_row_index,
    output_projector,
    lower_factor_weight,
    upper_factor_weight,
):
    seq_len = rotated_queries.shape[1]
    head_size = HEAD_WIDTH
    heads_dev = rotated_queries.shape[2] // head_size
    group_size = QUERY_HEAD_COUNT // KVH
    score_scale = head_size ** (-0.5)
    core = lax.axis_index("draft")
    tensor = lax.axis_index("tensor")
    dp = lax.axis_index("dp")
    upper_core = core == 1
    rank_index = tensor * 2 + core
    kv_head = rank_index * heads_dev // group_size
    width = output_projector.shape[1] // 2
    rank = lower_factor_weight.shape[1]

    core_ref = core.reshape(1)
    y = tensor // SIDE
    place = jnp.stack([core, y, kv_head]).astype(jnp.int32)
    rows, taps = output_gradient[0], draft_loss_gradients[0]
    queries, lower = rotated_queries[0], lower_factor_weight.T
    band, output_flattened, inner_piece, key_head, value_head, give = forward(
        place,
        queries,
        segment_labels,
        lower,
        rotated_keys[0],
        stored_values[0],
        rows,
        taps,
        upper_factor_weight,
        output_projector,
    )
    block, _, stacked = blend(
        place,
        tapped_row_index,
        rows,
        taps,
        upper_factor_weight,
        output_projector,
        swapped(give, "draft", 1),
        inner_piece,
    )
    z1, z2 = near_move(block, 1, 1), near_move(block, 3, 2)

    half = seq_len // 2
    own_far = spread(stacked, AXES, far_groups())
    quarter = ride_sum(own_far, seq_len)
    from_z = [first_swapped(quarter, mask).astype(F32) for mask in (1, 2, 3)]
    quarter = ((quarter.astype(F32) + from_z[1]) + (from_z[0] + from_z[2])).astype(BF16)
    low = near_move(jnp.where(upper_core, block[:half], z1[:half]), 1, 3)
    high = near_move(jnp.where(upper_core, block[half:], z2[half:]), 3, 3)
    last = jnp.concatenate([low, high], axis=0)
    near = jnp.concatenate([z1, z2, widened(quarter, SIDE)], axis=0)
    near_far = [far_move(near, k) for k in (1, 2, 3)]
    give, sums = give_near(
        place,
        after(quarter, last),
        [own_far, z1, z2, *near_far],
        [own_far.shape[0] // SIDE] + [seq_len] * 5,
        seq_len,
    )
    came_near = swapped(give, "draft", 1)
    residual = lax.dynamic_slice_in_dim(came_near, y * seq_len, seq_len, 0)
    residual = jnp.where(upper_core, residual, block[:, :width])
    last_far = [far_move(last, k) for k in (1, 2, 3)]
    sums = jnp.where(upper_core, narrowed(came_near[12 * seq_len :], 2), sums)
    adapter_inner, adapter_gradient = sums[:, :rank], sums[:, rank:]

    lower_piece = lax.dot_general(adapter_gradient, output_flattened, TN, preferred_element_type=F32)
    upper_piece = lax.dot_general(adapter_inner, residual, TN, preferred_element_type=F32)
    factor = jnp.concatenate([lower_piece, upper_piece], axis=0)
    factor = factor + swapped(factor, "dp", 1)
    from_dp = swapped(factor, "dp", 2)
    give = give_half(core_ref, [after(last, came_near, factor), *last_far], seq_len)
    came_last = swapped(give, "draft", 1)

    part_mine, part_other = frozen_product(
        core_ref,
        block_order(1 - core, dp, tensor),
        [(own_far, own_far.shape[0] // SIDE)]
        + [(a, seq_len) for a in (z1, z2, *near_far, last, *last_far)],
        [(came_near, seq_len), (came_last, seq_len)],
        seq_len,
    )
    factor = factor + after(from_dp, part_mine)
    came = swapped(after(part_other, factor), "draft", 1)
    from_dp = swapped(factor, "dp", 4)
    query_grad, keep, give = backward(
        core_ref,
        part_mine,
        came,
        sums,
        lower,
        band,
        output_flattened,
        queries,
        key_head,
        value_head,
    )
    factor = factor + after(from_dp, give)
    came = swapped(after(give, factor), "draft", 1)
    from_dp = swapped(factor, "dp", 8)
    keep, give = quarters_kept((tensor & 1).reshape(1), keep, came)
    came = swapped(give, "tensor", 1)
    factor = factor + after(from_dp, give)
    factor = factor * (adapter_scale / lax.axis_size("dp"))
    lower_gradient, upper_gradient = factor[:rank].T, factor[rank:]
    total = (keep + came.astype(F32)).astype(BF16)
    quarter = head_size // 4
    key_grad, value_grad = total[:quarter].T[None], total[quarter:].T[None]
    query_grad = query_grad[None]
    return (query_grad, key_grad, value_grad, lower_gradient, upper_gradient)


def solution(mesh):
    in_specs = (
        P("dp", None, ("tensor", "draft")),
        P("dp", None, None),
        P("dp", None, None),
        P("dp", None),
        P("dp", "draft", "tensor"),
        P("dp", "draft", "tensor"),
        P("dp", None),
        P(("tensor", "draft"), "dp"),
        P(("tensor", "draft"), None),
        P(None, ("tensor", "draft")),
    )
    out_specs = (
        P("dp", None, ("tensor", "draft")),
        P("dp", None, ("tensor", "draft")),
        P("dp", None, ("tensor", "draft")),
        P(("tensor", "draft"), None),
        P(None, ("tensor", "draft")),
    )
    return jax.shard_map(
        on_device, mesh=mesh, in_specs=in_specs, out_specs=out_specs, check_vma=False
    )
```

```python
import functools

import jax
import jax.numpy as jnp
from jax import lax
from jax.experimental import pallas as pl
from jax.experimental.pallas import tpu as pltpu
from jax.sharding import PartitionSpec as P

QUERY_HEAD_COUNT = 64
KVH = 8
HEAD_WIDTH = 128
SIDE = 4
SEGMENT_MOST = 128
ROOMY = pltpu.CompilerParams(vmem_limit_bytes=16 * 1024 * 1024)

adapter_scale = 2.0

F32, BF16 = jnp.float32, jnp.bfloat16
NT = (((1,), (1,)), ((), ()))
TN = (((0,), (0,)), ((), ()))


AXES = ("dp", "tensor", "draft")


def moved(array, residual_to, slab_to):
    n_dp, n_tensor = lax.axis_size("dp"), lax.axis_size("tensor")
    pairs = []
    for d in range(n_dp):
        for t in range(n_tensor):
            at = (d * n_tensor + t) * 2
            pairs.append((at, (d * n_tensor + residual_to(t)) * 2))
            pairs.append((at + 1, (slab_to(d) * n_tensor + t) * 2 + 1))
    return lax.ppermute(array, AXES, pairs)


def spread(stacked, axes, groups):
    return lax.all_to_all(stacked, axes, 0, 0, axis_index_groups=groups, tiled=True)


def high_groups():
    return [[i * SIDE + j for i in range(SIDE)] for j in range(SIDE)]


def far_groups():
    n_dp, n_tensor = lax.axis_size("dp"), lax.axis_size("tensor")
    groups = []
    for one in high_groups():
        groups += [[(d * n_tensor + t) * 2 for t in one] for d in range(n_dp)]
        groups += [[(d * n_tensor + t) * 2 + 1 for d in one] for t in range(n_tensor)]
    return groups


def far_move(array, k):
    step = lambda i: (i + k * SIDE) % (SIDE * SIDE)
    return moved(array, step, step)


def near_move(array, shift, mask):
    ahead = lambda t: t // SIDE * SIDE + (t + shift) % SIDE
    return moved(array, ahead, lambda d: d ^ mask)


def first_swapped(array, mask):
    n = lax.axis_size("dp") * lax.axis_size("tensor")
    return lax.ppermute(array, AXES, [(2 * i, 2 * (i ^ mask)) for i in range(n)])


def swapped(array, axis, mask):
    return lax.ppermute(array, axis, [(i, i ^ mask) for i in range(lax.axis_size(axis))])


def after(array, *earlier):
    return lax.optimization_barrier((array, *earlier))[0]


def blend_kernel(
    place_ref, tapped_ref, rows_ref, taps_ref, upper_ref, slab_ref, came_ref, inner_ref,
    block_ref, sums_ref, stack_ref,
):
    n, n_taps, rank = rows_ref.shape[0], taps_ref.shape[0], upper_ref.shape[0]
    width = upper_ref.shape[1]
    at_upper = n + n_taps
    at_inner = at_upper + rank // 2

    @pl.when(place_ref[0] == 0)
    def _():
        taps = jnp.concatenate([taps_ref[...], came_ref[n:at_upper]], axis=0)
        place = lax.broadcasted_iota(jnp.int32, (2 * n, 2 * n_taps), 0)
        hit = jnp.where(place == tapped_ref[...], 1.0, 0.0).astype(BF16)
        spread = jnp.dot(hit, taps, preferred_element_type=F32)
        block_ref[:n] = (rows_ref[...].astype(F32) + spread[:n]).astype(BF16)
        block_ref[n:] = (came_ref[:n].astype(F32) + spread[n:]).astype(BF16)
        upper = came_ref[at_upper:at_inner]
        upper = jnp.concatenate([upper[:, :width], upper[:, width:]], axis=0)
        lora = lax.dot_general(
            block_ref[:, :width], upper_ref[...], NT, preferred_element_type=F32
        ) + lax.dot_general(block_ref[:, width:], upper, NT, preferred_element_type=F32)
        inner = came_ref[at_inner:].astype(F32)
        inner = [inner[:, i * rank : (i + 1) * rank] for i in range(inner.shape[1] // rank)]
        inner = inner_ref[...] + jnp.concatenate(inner, axis=0)
        sums_ref[...] = jnp.concatenate([inner, lora], axis=1)

    @pl.when(place_ref[0] == 1)
    def _():
        block_ref[:n] = came_ref[:n]
        block_ref[n:] = slab_ref[...]
        sums_ref[...] = jnp.zeros_like(sums_ref)

    quarter = 2 * n // SIDE
    step = stack_ref.shape[0] // SIDE
    for i in range(SIDE):
        at = i * step
        stack_ref[at : at + 2 * n] = block_ref[...]
        share = sums_ref[i * quarter : (i + 1) * quarter].astype(BF16)
        stack_ref[at + 2 * n : at + step] = jnp.concatenate(
            jnp.split(share, SIDE, axis=0), axis=1
        )


def blend(place, tapped, rows, taps, upper, slab, came, inner):
    n, width = rows.shape
    ride = 2 * n // SIDE * 2 * upper.shape[0] // width
    vmem = pl.BlockSpec(memory_space=pltpu.VMEM)
    return pl.pallas_call(
        blend_kernel,
        out_shape=(
            jax.ShapeDtypeStruct((2 * n, width), BF16),
            jax.ShapeDtypeStruct((2 * n, 2 * upper.shape[0]), F32),
            jax.ShapeDtypeStruct((SIDE * (2 * n + ride), width), BF16),
        ),
        in_specs=[pl.BlockSpec(memory_space=pltpu.SMEM)] + [vmem] * 7,
        out_specs=(vmem,) * 3,
        compiler_params=ROOMY,
        name="blend",
    )(place, tapped, rows, taps, upper, slab, came, inner)


def widened(array, n):
    return jnp.concatenate(jnp.split(array, n, axis=0), axis=1)


def narrowed(array, n):
    return jnp.concatenate(jnp.split(array, n, axis=1), axis=0)


def ride_sum_kernel(rows, stack_ref, out_ref, rides, sems):
    n_ride = rides.shape[1]
    copies = []
    for i in range(SIDE):
        ride = stack_ref.at[pl.ds(i * (rows + n_ride) + rows, n_ride)]
        copies.append(pltpu.make_async_copy(ride, rides.at[i], sems.at[i]))
        copies[-1].start()
    for copy in copies:
        copy.wait()
    total = rides[0].astype(F32)
    for i in range(1, SIDE):
        total = total + rides[i].astype(F32)
    out_ref[...] = jnp.concatenate(jnp.split(total.astype(BF16), SIDE, axis=1), axis=0)


def ride_sum(stack, rows):
    n_ride, width = stack.shape[0] // SIDE - rows, stack.shape[1]
    return pl.pallas_call(
        functools.partial(ride_sum_kernel, rows),
        out_shape=jax.ShapeDtypeStruct((n_ride * SIDE, width // SIDE), BF16),
        in_specs=[pl.BlockSpec(memory_space=pl.ANY)],
        out_specs=pl.BlockSpec(memory_space=pltpu.VMEM),
        scratch_shapes=[
            pltpu.VMEM((SIDE, n_ride, width), BF16),
            pltpu.SemaphoreType.DMA((SIDE,)),
        ],
        compiler_params=ROOMY,
        name="ride_sum",
    )(stack)


def give_copies(parts, other, sources, out_ref, sems):
    width = out_ref.shape[1]
    columns = pl.ds(pl.multiple_of(other * width, width), width)
    copies, at = [], 0
    for i, (which, row, n) in enumerate(parts):
        source = sources[which].at[pl.ds(row, n), columns]
        copies.append(pltpu.make_async_copy(source, out_ref.at[pl.ds(at, n)], sems.at[i]))
        copies[-1].start()
        at += n
    return copies


def give_kernel(parts, core_ref, *refs):
    sources, (out_ref, sems) = refs[:-2], refs[-2:]
    for copy in give_copies(parts, 1 - core_ref[0], sources, out_ref, sems):
        copy.wait()


def give_half(core, arrays, rows):
    any_spec = pl.BlockSpec(memory_space=pl.ANY)
    parts = [(i, at, rows) for i, a in enumerate(arrays) for at in range(0, a.shape[0], rows)]
    return pl.pallas_call(
        functools.partial(give_kernel, parts),
        out_shape=jax.ShapeDtypeStruct((len(parts) * rows, arrays[0].shape[1] // 2), BF16),
        in_specs=[pl.BlockSpec(memory_space=pltpu.SMEM)] + [any_spec] * len(arrays),
        out_specs=pl.BlockSpec(memory_space=pltpu.VMEM),
        scratch_shapes=[pltpu.SemaphoreType.DMA((len(parts),))],
        compiler_params=ROOMY,
        name="give",
    )(core, *arrays)


def give_near_kernel(parts, at_ride, place_ref, quarter_ref, *refs):
    sources, (out_ref, sums_ref, rides, sems) = refs[:-4], refs[-4:]
    copies = give_copies(parts, 1 - place_ref[0], sources, out_ref, sems)
    for k, far in enumerate(sources[-3:]):
        ride = far.at[pl.ds(at_ride, rides.shape[1])]
        copies.append(pltpu.make_async_copy(ride, rides.at[k], sems.at[len(parts) + k]))
        copies[-1].start()
    n = quarter_ref.shape[0]
    sums_ref[pl.ds(pl.multiple_of(place_ref[1] * n, n), n)] = quarter_ref[...]
    for copy in copies:
        copy.wait()
    for k in range(3):
        source = (place_ref[1] + SIDE - 1 - k) % SIDE
        ride = jnp.concatenate(jnp.split(rides[k], SIDE, axis=1), axis=0)
        sums_ref[pl.ds(pl.multiple_of(source * n, n), n)] = ride
    at = sum(part[2] for part in parts)
    out_ref[at:] = jnp.concatenate(jnp.split(sums_ref[...], 2, axis=0), axis=1)


def give_near(place, quarter, arrays, steps, rows):
    width = arrays[0].shape[1]
    at_ride = arrays[-1].shape[0] // rows * rows
    n_ride = arrays[-1].shape[0] - at_ride
    n, columns = quarter.shape
    parts = [
        (i, at, rows)
        for i, (a, step) in enumerate(zip(arrays, steps))
        for at in range(0, a.shape[0] - rows + 1, step)
    ]
    vmem, any_spec = pl.BlockSpec(memory_space=pltpu.VMEM), pl.BlockSpec(memory_space=pl.ANY)
    n_sums = SIDE * n * columns * 2 // width
    return pl.pallas_call(
        functools.partial(give_near_kernel, parts, at_ride),
        out_shape=(
            jax.ShapeDtypeStruct((len(parts) * rows + n_sums, width // 2), BF16),
            jax.ShapeDtypeStruct((SIDE * n, columns), BF16),
        ),
        in_specs=[pl.BlockSpec(memory_space=pltpu.SMEM), vmem] + [any_spec] * len(arrays),
        out_specs=(vmem,) * 2,
        scratch_shapes=[
            pltpu.VMEM((3, n_ride, width), BF16),
            pltpu.SemaphoreType.DMA((len(parts) + 3,)),
        ],
        compiler_params=ROOMY,
        name="give_near",
    )(place, quarter, *arrays)


def frozen_kernel(n_held, parts, core_ref, place_ref, *refs):
    sources, (mine, other, own, came, sems) = refs[:-5], refs[-5:]
    rows, cols = mine.shape
    blocks = len(parts) // 2
    width = own.shape[1] // blocks
    columns = pl.ds(pl.multiple_of(core_ref[0] * width, width), width)
    copies = []
    for i, (which, row) in enumerate(parts):
        if i < blocks:
            target = own.at[:, pl.ds(i * width, width)]
        else:
            at = pl.multiple_of(place_ref[i - blocks] * width, width)
            target = came.at[:, pl.ds(at, width)]
        source = sources[which].at[pl.ds(row, rows), columns if which < n_held else pl.ds(0, width)]
        copies.append(pltpu.make_async_copy(source, target, sems.at[i]))
    for copy in copies[blocks:] + copies[:blocks]:
        copy.start()
    for copy in copies[blocks:]:
        copy.wait()
    together = blocks // 4

    def total(first, second):
        result = None
        for i in range(0, blocks, together):
            for copy in copies[i : i + together]:
                copy.wait()
            depth = slice(i * width, (i + together) * width)
            term = lax.dot_general(
                first[:, depth], second[:, depth], NT, preferred_element_type=F32
            )
            result = term if result is None else result + term
        return result

    @pl.when(core_ref[0] == 0)
    def _():
        product = total(own, came)
        mine[...] = product[:, :cols]
        other[...] = product[:, cols:]

    @pl.when(core_ref[0] == 1)
    def _():
        product = total(came, own)
        mine[...] = product[:, cols:]
        other[...] = product[:, :cols]


def frozen_product(core, place, own, came, rows):
    arrays = [a for a, _ in (*own, *came)]
    parts = []
    for i, (a, step) in enumerate((*own, *came)):
        parts += [(i, at) for at in range(0, a.shape[0] - rows + 1, step)]
    width = came[0][0].shape[1]
    held = pltpu.VMEM((rows, len(parts) // 2 * width), BF16)
    return pl.pallas_call(
        functools.partial(frozen_kernel, len(own), parts),
        out_shape=(jax.ShapeDtypeStruct((rows, rows // 2), F32),) * 2,
        in_specs=[pl.BlockSpec(memory_space=pltpu.SMEM)] * 2
        + [pl.BlockSpec(memory_space=pl.ANY)] * len(arrays),
        out_specs=(pl.BlockSpec(memory_space=pltpu.VMEM),) * 2,
        scratch_shapes=[held, held, pltpu.SemaphoreType.DMA((len(parts),))],
        compiler_params=pltpu.CompilerParams(vmem_limit_bytes=56 * 1024 * 1024),
        cost_estimate=pl.CostEstimate(
            flops=4 * rows * rows * held.shape[1], bytes_accessed=24 << 20, transcendentals=0
        ),
        name="frozen",
    )(core, place, *arrays)


def block_order(core, dp, tensor):
    stage = jnp.array([0] * 4 + [1, 2] * 4 + [3] * 4, jnp.int32)
    step = jnp.array([0, 1, 2, 3, 0, 0, 1, 1, 2, 2, 3, 3, 0, 1, 2, 3], jnp.int32)
    first = core == 0
    mine, theirs = jnp.where(first, tensor, dp) // SIDE, jnp.where(first, dp, tensor) // SIDE
    high = jnp.where(stage == 0, step, (mine - step) % SIDE)
    shift = jnp.where(stage == 2, 3, jnp.where(stage == 3, 2, stage))
    low = jnp.where(first, (tensor - shift) % SIDE, (dp % SIDE) ^ stage)
    back = (tensor - low) % SIDE
    back = jnp.where(back == 2, 3, jnp.where(back == 3, 2, back))
    stage = jnp.where(first, (dp % SIDE) ^ low, back)
    step = (theirs - high) % SIDE
    return jnp.where(
        stage == 0, high, jnp.where(stage == 3, 12 + step, 3 + stage + 2 * step)
    )


def window(i, rows):
    return max(i - 1, 0) * rows


def forward_kernel(
    scale, place_ref, q_ref, label_ref, lower_ref, keys_ref, values_ref, rows_ref, taps_ref,
    upper_ref, slab_ref, band_ref, out_ref, inner_ref, k_ref, v_ref, give_ref, sems,
):
    head = k_ref.shape[1]
    n, n_taps, (rank, width) = rows_ref.shape[0], taps_ref.shape[0], upper_ref.shape
    at_upper = n + n_taps
    at_inner = at_upper + rank // 2
    mine = pl.ds(pl.multiple_of(place_ref[2] * head, head), head)

    def copy(i, source, target):
        return pltpu.make_async_copy(source, target, sems.at[i])

    seen = [copy(0, keys_ref.at[:, mine], k_ref), copy(1, values_ref.at[:, mine], v_ref)]
    given = [copy(2, taps_ref, give_ref.at[pl.ds(n, n_taps)])]
    for i in range(2):
        target = give_ref.at[pl.ds(at_upper, rank // 2), pl.ds(i * width, width)]
        given.append(copy(3 + i, upper_ref.at[pl.ds(i * (rank // 2), rank // 2)], target))
    for one in seen + given:
        one.start()

    @pl.when(place_ref[0] == 0)
    def _():
        copy(5, slab_ref, give_ref.at[pl.ds(0, n)]).start()

    @pl.when(place_ref[0] == 1)
    def _():
        copy(5, rows_ref, give_ref.at[pl.ds(0, n)]).start()

    for one in seen:
        one.wait()
    rows = band_ref.shape[2] // 2
    labels = label_ref[...].astype(F32)
    ahead = lax.broadcasted_iota(jnp.int32, (rows, 2 * rows), 0)
    ahead = ahead - lax.broadcasted_iota(jnp.int32, (rows, 2 * rows), 1)
    tiles = [(i, h) for i in range(q_ref.shape[0] // rows) for h in range(band_ref.shape[0])]
    scores = {}
    for i, h in tiles:
        at, low = i * rows, window(i, rows)
        scores[i, h] = lax.dot_general(
            q_ref[at : at + rows, h * head : (h + 1) * head],
            k_ref[low : low + 2 * rows],
            NT,
            preferred_element_type=F32,
        )
    allowed = {}
    for i in range(q_ref.shape[0] // rows):
        at, low = i * rows, window(i, rows)
        own = jnp.broadcast_to(labels[:, at : at + rows], (rows, rows)).T
        own = jnp.concatenate([own, own], axis=1)
        allowed[i] = (ahead >= low - at) & (own == labels[:, low : low + 2 * rows])
    probs = {}
    for i, h in tiles:
        masked = jnp.where(allowed[i], scores[i, h] * scale, -jnp.inf)
        raised = jnp.exp(masked - jnp.max(masked, axis=1, keepdims=True))
        probs[i, h] = raised / jnp.sum(raised, axis=1, keepdims=True)
    outs = {}
    for i, h in tiles:
        low = window(i, rows)
        outs[i, h] = jnp.dot(
            probs[i, h].astype(BF16), v_ref[low : low + 2 * rows], preferred_element_type=F32
        ).astype(BF16)
    for i, h in tiles:
        at = i * rows
        band_ref[h, at : at + rows] = probs[i, h]
        out_ref[at : at + rows, h * head : (h + 1) * head] = outs[i, h]
    inner = lax.dot_general(out_ref[...], lower_ref[...], NT, preferred_element_type=F32)
    inner_ref[...] = inner
    inner = jnp.split(inner.astype(BF16), 2 * width // rank, axis=0)
    give_ref[at_inner:] = jnp.concatenate(inner, axis=1)
    for one in given:
        one.wait()
    copy(5, rows_ref, give_ref.at[pl.ds(0, n)]).wait()


def forward(place, queries, labels, lower, keys, values, rows, taps, upper, slab):
    n, width = queries.shape
    heads, rank = width // HEAD_WIDTH, lower.shape[0]
    any_spec = pl.BlockSpec(memory_space=pl.ANY)
    vmem = pl.BlockSpec(memory_space=pltpu.VMEM)
    n_give = rows.shape[0] + taps.shape[0] + rank // 2 + n * rank // rows.shape[1]
    return pl.pallas_call(
        functools.partial(forward_kernel, HEAD_WIDTH**-0.5),
        out_shape=(
            jax.ShapeDtypeStruct((heads, n, 2 * SEGMENT_MOST), F32),
            jax.ShapeDtypeStruct((n, width), BF16),
            jax.ShapeDtypeStruct((n, rank), F32),
            jax.ShapeDtypeStruct((n, HEAD_WIDTH), BF16),
            jax.ShapeDtypeStruct((n, HEAD_WIDTH), BF16),
            jax.ShapeDtypeStruct((n_give, rows.shape[1]), BF16),
        ),
        in_specs=[pl.BlockSpec(memory_space=pltpu.SMEM)] + [vmem] * 3 + [any_spec] * 6,
        out_specs=(vmem,) * 6,
        scratch_shapes=[pltpu.SemaphoreType.DMA((6,))],
        name="attention",
    )(place, queries, labels, lower, keys, values, rows, taps, upper, slab)


def backward_kernel(
    scale, core_ref, mine_ref, came_ref, adapter_ref, lower_ref, band_ref, out_ref, q_ref, k_ref,
    v_ref, query_ref, keep_ref, give_ref, key_sum, value_sum,
):
    rows = band_ref.shape[2] // 2
    head = k_ref.shape[1]
    n = q_ref.shape[0] // rows
    tiles = [(i, h) for i in range(n) for h in range(band_ref.shape[0])]

    def part(i):
        return slice(i * rows, (i + 1) * rows)

    def seen(i):
        return slice(window(i, rows), window(i, rows) + 2 * rows)

    def cols(h):
        return slice(h * head, (h + 1) * head)

    adapter = adapter_ref[:, lower_ref.shape[0] :]
    lora = jnp.dot(adapter, lower_ref[...], preferred_element_type=F32)
    gradient = (mine_ref[...] + came_ref[...] + adapter_scale * lora).astype(BF16)
    own = {(i, h): gradient[part(i), cols(h)] for i, h in tiles}
    prob_grad, terms, score_grad = {}, {}, {}
    for i, h in tiles:
        prob_grad[i, h] = lax.dot_general(
            own[i, h], v_ref[seen(i)], NT, preferred_element_type=F32
        )
    for i, h in tiles:
        product = own[i, h].astype(F32) * out_ref[part(i), cols(h)].astype(F32)
        terms[i, h] = jnp.sum(product, axis=1, keepdims=True)
    probs = {(i, h): band_ref[h, part(i)] for i, h in tiles}
    for i, h in tiles:
        score_grad[i, h] = (probs[i, h] * (prob_grad[i, h] - terms[i, h])).astype(BF16)
    for i, h in tiles:
        query_grad = jnp.dot(score_grad[i, h], k_ref[seen(i)], preferred_element_type=F32)
        query_ref[part(i), cols(h)] = (scale * query_grad).astype(BF16)
    for j in range(n):
        sees = [(j, 0 if j == 0 else 1)] + [(i, 0) for i in (j + 1,) if i < n]
        key_total, value_total = None, None
        for i, side in sees:
            for h in range(band_ref.shape[0]):
                key_part = lax.dot_general(
                    q_ref[part(i), cols(h)], score_grad[i, h][:, part(side)], TN,
                    preferred_element_type=F32,
                )
                value_part = lax.dot_general(
                    own[i, h], probs[i, h][:, part(side)].astype(BF16), TN,
                    preferred_element_type=F32,
                )
                key_total = key_part if key_total is None else key_total + key_part
                value_total = value_part if value_total is None else value_total + value_part
        key_sum[:, part(j)] = key_total
        value_sum[:, part(j)] = value_total
    quarter = head // 4
    first = core_ref[0] == 0
    for source, factor, at in ((key_sum, scale, 0), (value_sum, None, 2 * quarter)):
        total = source[...] if factor is None else source[...] * factor
        for i in (0, 1):
            even = total[2 * i * quarter : (2 * i + 1) * quarter]
            odd = total[(2 * i + 1) * quarter : (2 * i + 2) * quarter]
            rows = slice(at + i * quarter, at + (i + 1) * quarter)
            keep_ref[rows] = jnp.where(first, even, odd)
            give_ref[rows] = jnp.where(first, odd, even)


def backward(core, mine, came, adapter, lower, band, out, queries, key_head, value_head):
    n, width = queries.shape
    half = jax.ShapeDtypeStruct((HEAD_WIDTH, n), F32)
    return pl.pallas_call(
        functools.partial(backward_kernel, HEAD_WIDTH**-0.5),
        out_shape=(jax.ShapeDtypeStruct((n, width), BF16), half, half),
        in_specs=[pl.BlockSpec(memory_space=pltpu.SMEM)]
        + [pl.BlockSpec(memory_space=pltpu.VMEM)] * 9,
        out_specs=(pl.BlockSpec(memory_space=pltpu.VMEM),) * 3,
        scratch_shapes=[pltpu.VMEM((HEAD_WIDTH, n), F32)] * 2,
        cost_estimate=pl.CostEstimate(
            flops=20 * n * width * 2 * SEGMENT_MOST, bytes_accessed=16 << 20, transcendentals=0
        ),
        compiler_params=ROOMY,
        name="attention_gradient",
    )(core, mine, came, adapter, lower, band, out, queries, key_head, value_head)


def quarters_kernel(chip_ref, keep_ref, came_ref, out_ref, give_ref):
    quarter = keep_ref.shape[0] // 4
    first = chip_ref[0] == 0
    for i in (0, 1):
        at = 2 * i * quarter
        even = keep_ref[at : at + quarter] + came_ref[at : at + quarter]
        odd = keep_ref[at + quarter : at + 2 * quarter] + came_ref[at + quarter : at + 2 * quarter]
        rows = slice(i * quarter, (i + 1) * quarter)
        out_ref[rows] = jnp.where(first, even, odd)
        give_ref[rows] = jnp.where(first, odd, even).astype(BF16)


def quarters_kept(chip, keep, came):
    n, width = keep.shape
    return pl.pallas_call(
        quarters_kernel,
        out_shape=(
            jax.ShapeDtypeStruct((n // 2, width), F32),
            jax.ShapeDtypeStruct((n // 2, width), BF16),
        ),
        in_specs=[pl.BlockSpec(memory_space=pltpu.SMEM)]
        + [pl.BlockSpec(memory_space=pltpu.VMEM)] * 2,
        out_specs=(pl.BlockSpec(memory_space=pltpu.VMEM),) * 2,
        compiler_params=ROOMY,
        name="quarters",
    )(chip, keep, came)


def on_device(
    rotated_queries,
    rotated_keys,
    stored_values,
    segment_labels,
    output_gradient,
    draft_loss_gradients,
    tapped_row_index,
    output_projector,
    lower_factor_weight,
    upper_factor_weight,
):
    seq_len = rotated_queries.shape[1]
    head_size = HEAD_WIDTH
    heads_dev = rotated_queries.shape[2] // head_size
    group_size = QUERY_HEAD_COUNT // KVH
    score_scale = head_size ** (-0.5)
    core = lax.axis_index("draft")
    tensor = lax.axis_index("tensor")
    dp = lax.axis_index("dp")
    upper_core = core == 1
    rank_index = tensor * 2 + core
    kv_head = rank_index * heads_dev // group_size
    width = output_projector.shape[1] // 2
    rank = lower_factor_weight.shape[1]

    core_ref = core.reshape(1)
    y = tensor // SIDE
    place = jnp.stack([core, y, kv_head]).astype(jnp.int32)
    rows, taps = output_gradient[0], draft_loss_gradients[0]
    queries, lower = rotated_queries[0], lower_factor_weight.T
    band, output_flattened, inner_piece, key_head, value_head, give = forward(
        place,
        queries,
        segment_labels,
        lower,
        rotated_keys[0],
        stored_values[0],
        rows,
        taps,
        upper_factor_weight,
        output_projector,
    )
    block, _, stacked = blend(
        place,
        tapped_row_index,
        rows,
        taps,
        upper_factor_weight,
        output_projector,
        swapped(give, "draft", 1),
        inner_piece,
    )
    z1, z2 = near_move(block, 1, 1), near_move(block, 3, 2)

    half = seq_len // 2
    own_far = spread(stacked, AXES, far_groups())
    quarter = ride_sum(own_far, seq_len)
    from_z = [first_swapped(quarter, mask).astype(F32) for mask in (1, 2, 3)]
    quarter = ((quarter.astype(F32) + from_z[1]) + (from_z[0] + from_z[2])).astype(BF16)
    low = near_move(jnp.where(upper_core, block[:half], z1[:half]), 1, 3)
    high = near_move(jnp.where(upper_core, block[half:], z2[half:]), 3, 3)
    last = jnp.concatenate([low, high], axis=0)
    near = jnp.concatenate([z1, z2, widened(quarter, SIDE)], axis=0)
    near_far = [far_move(near, k) for k in (1, 2, 3)]
    give, sums = give_near(
        place,
        after(quarter, last),
        [own_far, z1, z2, *near_far],
        [own_far.shape[0] // SIDE] + [seq_len] * 5,
        seq_len,
    )
    came_near = swapped(give, "draft", 1)
    residual = lax.dynamic_slice_in_dim(came_near, y * seq_len, seq_len, 0)
    residual = jnp.where(upper_core, residual, block[:, :width])
    last_far = [far_move(last, k) for k in (1, 2, 3)]
    sums = jnp.where(upper_core, narrowed(came_near[12 * seq_len :], 2), sums)
    adapter_inner, adapter_gradient = sums[:, :rank], sums[:, rank:]

    lower_piece = lax.dot_general(adapter_gradient, output_flattened, TN, preferred_element_type=F32)
    upper_piece = lax.dot_general(adapter_inner, residual, TN, preferred_element_type=F32)
    factor = jnp.concatenate([lower_piece, upper_piece], axis=0)
    factor = factor + swapped(factor, "dp", 1)
    from_dp = swapped(factor, "dp", 2)
    give = give_half(core_ref, [after(last, came_near, factor), *last_far], seq_len)
    came_last = swapped(give, "draft", 1)

    part_mine, part_other = frozen_product(
        core_ref,
        block_order(1 - core, dp, tensor),
        [(own_far, own_far.shape[0] // SIDE)]
        + [(a, seq_len) for a in (z1, z2, *near_far, last, *last_far)],
        [(came_near, seq_len), (came_last, seq_len)],
        seq_len,
    )
    factor = factor + after(from_dp, part_mine)
    came = swapped(after(part_other, factor), "draft", 1)
    from_dp = swapped(factor, "dp", 4)
    query_grad, keep, give = backward(
        core_ref,
        part_mine,
        came,
        sums,
        lower,
        band,
        output_flattened,
        queries,
        key_head,
        value_head,
    )
    factor = factor + after(from_dp, give)
    came = swapped(after(give, factor), "draft", 1)
    from_dp = swapped(factor, "dp", 8)
    keep, give = quarters_kept((tensor & 1).reshape(1), keep, came)
    came = swapped(give, "tensor", 1)
    factor = factor + after(from_dp, give)
    factor = factor * (adapter_scale / lax.axis_size("dp"))
    lower_gradient, upper_gradient = factor[:rank].T, factor[rank:]
    total = (keep + came.astype(F32)).astype(BF16)
    quarter = head_size // 4
    key_grad, value_grad = total[:quarter].T[None], total[quarter:].T[None]
    query_grad = query_grad[None]
    return (query_grad, key_grad, value_grad, lower_gradient, upper_gradient)


def solution(mesh):
    in_specs = (
        P("dp", None, ("tensor", "draft")),
        P("dp", None, None),
        P("dp", None, None),
        P("dp", None),
        P("dp", "draft", "tensor"),
        P("dp", "draft", "tensor"),
        P("dp", None),
        P(("tensor", "draft"), "dp"),
        P(("tensor", "draft"), None),
        P(None, ("tensor", "draft")),
    )
    out_specs = (
        P("dp", None, ("tensor", "draft")),
        P("dp", None, ("tensor", "draft")),
        P("dp", None, ("tensor", "draft")),
        P(("tensor", "draft"), None),
        P(None, ("tensor", "draft")),
    )
    return jax.shard_map(
        on_device, mesh=mesh, in_specs=in_specs, out_specs=out_specs, check_vma=False
    )
```

```python
import functools

import jax
import jax.numpy as jnp
from jax import lax
from jax.experimental import pallas as pl
from jax.experimental.pallas import tpu as pltpu
from jax.sharding import PartitionSpec as P

QUERY_HEAD_COUNT = 64
KVH = 8
HEAD_WIDTH = 128
SIDE = 4
SEGMENT_MOST = 128
ROOMY = pltpu.CompilerParams(vmem_limit_bytes=16 * 1024 * 1024)

adapter_scale = 2.0

F32, BF16 = jnp.float32, jnp.bfloat16
NT = (((1,), (1,)), ((), ()))
TN = (((0,), (0,)), ((), ()))


AXES = ("dp", "tensor", "draft")


def moved(array, residual_to, slab_to):
    n_dp, n_tensor = lax.axis_size("dp"), lax.axis_size("tensor")
    pairs = []
    for d in range(n_dp):
        for t in range(n_tensor):
            at = (d * n_tensor + t) * 2
            pairs.append((at, (d * n_tensor + residual_to(t)) * 2))
            pairs.append((at + 1, (slab_to(d) * n_tensor + t) * 2 + 1))
    return lax.ppermute(array, AXES, pairs)


def spread(stacked, axes, groups):
    return lax.all_to_all(stacked, axes, 0, 0, axis_index_groups=groups, tiled=True)


def high_groups():
    return [[i * SIDE + j for i in range(SIDE)] for j in range(SIDE)]


def far_groups():
    n_dp, n_tensor = lax.axis_size("dp"), lax.axis_size("tensor")
    groups = []
    for one in high_groups():
        groups += [[(d * n_tensor + t) * 2 for t in one] for d in range(n_dp)]
        groups += [[(d * n_tensor + t) * 2 + 1 for d in one] for t in range(n_tensor)]
    return groups


def far_move(array, k):
    step = lambda i: (i + k * SIDE) % (SIDE * SIDE)
    return moved(array, step, step)


def in_step_order(arrays):
    return [arrays[1], arrays[0], arrays[2]]


def near_move(array, shift, mask):
    ahead = lambda t: t // SIDE * SIDE + (t + shift) % SIDE
    return moved(array, ahead, lambda d: d ^ mask)


def first_swapped(array, mask):
    n = lax.axis_size("dp") * lax.axis_size("tensor")
    return lax.ppermute(array, AXES, [(2 * i, 2 * (i ^ mask)) for i in range(n)])


def swapped(array, axis, mask):
    return lax.ppermute(array, axis, [(i, i ^ mask) for i in range(lax.axis_size(axis))])


def after(array, *earlier):
    return lax.optimization_barrier((array, *earlier))[0]


def blend_kernel(
    place_ref, tapped_ref, rows_ref, taps_ref, upper_ref, slab_ref, came_ref, inner_ref,
    block_ref, sums_ref, stack_ref,
):
    n, n_taps, rank = rows_ref.shape[0], taps_ref.shape[0], upper_ref.shape[0]
    width = upper_ref.shape[1]
    at_upper = n + n_taps
    at_inner = at_upper + rank // 2

    @pl.when(place_ref[0] == 0)
    def _():
        taps = jnp.concatenate([taps_ref[...], came_ref[n:at_upper]], axis=0)
        place = lax.broadcasted_iota(jnp.int32, (2 * n, 2 * n_taps), 0)
        hit = jnp.where(place == tapped_ref[...], 1.0, 0.0).astype(BF16)
        spread = jnp.dot(hit, taps, preferred_element_type=F32)
        block_ref[:n] = (rows_ref[...].astype(F32) + spread[:n]).astype(BF16)
        block_ref[n:] = (came_ref[:n].astype(F32) + spread[n:]).astype(BF16)
        upper = came_ref[at_upper:at_inner]
        upper = jnp.concatenate([upper[:, :width], upper[:, width:]], axis=0)
        lora = lax.dot_general(
            block_ref[:, :width], upper_ref[...], NT, preferred_element_type=F32
        ) + lax.dot_general(block_ref[:, width:], upper, NT, preferred_element_type=F32)
        inner = came_ref[at_inner:].astype(F32)
        inner = [inner[:, i * rank : (i + 1) * rank] for i in range(inner.shape[1] // rank)]
        inner = inner_ref[...] + jnp.concatenate(inner, axis=0)
        sums_ref[...] = jnp.concatenate([inner, lora], axis=1)

    @pl.when(place_ref[0] == 1)
    def _():
        block_ref[:n] = came_ref[:n]
        block_ref[n:] = slab_ref[...]
        sums_ref[...] = jnp.zeros_like(sums_ref)

    quarter = 2 * n // SIDE
    step = stack_ref.shape[0] // SIDE
    for i in range(SIDE):
        at = i * step
        stack_ref[at : at + 2 * n] = block_ref[...]
        share = sums_ref[i * quarter : (i + 1) * quarter].astype(BF16)
        stack_ref[at + 2 * n : at + step] = jnp.concatenate(
            jnp.split(share, SIDE, axis=0), axis=1
        )


def blend(place, tapped, rows, taps, upper, slab, came, inner):
    n, width = rows.shape
    ride = 2 * n // SIDE * 2 * upper.shape[0] // width
    vmem = pl.BlockSpec(memory_space=pltpu.VMEM)
    return pl.pallas_call(
        blend_kernel,
        out_shape=(
            jax.ShapeDtypeStruct((2 * n, width), BF16),
            jax.ShapeDtypeStruct((2 * n, 2 * upper.shape[0]), F32),
            jax.ShapeDtypeStruct((SIDE * (2 * n + ride), width), BF16),
        ),
        in_specs=[pl.BlockSpec(memory_space=pltpu.SMEM)] + [vmem] * 7,
        out_specs=(vmem,) * 3,
        compiler_params=ROOMY,
        name="blend",
    )(place, tapped, rows, taps, upper, slab, came, inner)


def widened(array, n):
    return jnp.concatenate(jnp.split(array, n, axis=0), axis=1)


def narrowed(array, n):
    return jnp.concatenate(jnp.split(array, n, axis=1), axis=0)


def ride_sum_kernel(rows, stack_ref, out_ref, rides, sems):
    n_ride = rides.shape[1]
    copies = []
    for i in range(SIDE):
        ride = stack_ref.at[pl.ds(i * (rows + n_ride) + rows, n_ride)]
        copies.append(pltpu.make_async_copy(ride, rides.at[i], sems.at[i]))
        copies[-1].start()
    for copy in copies:
        copy.wait()
    total = rides[0].astype(F32)
    for i in range(1, SIDE):
        total = total + rides[i].astype(F32)
    out_ref[...] = jnp.concatenate(jnp.split(total.astype(BF16), SIDE, axis=1), axis=0)


def ride_sum(stack, rows):
    n_ride, width = stack.shape[0] // SIDE - rows, stack.shape[1]
    return pl.pallas_call(
        functools.partial(ride_sum_kernel, rows),
        out_shape=jax.ShapeDtypeStruct((n_ride * SIDE, width // SIDE), BF16),
        in_specs=[pl.BlockSpec(memory_space=pl.ANY)],
        out_specs=pl.BlockSpec(memory_space=pltpu.VMEM),
        scratch_shapes=[
            pltpu.VMEM((SIDE, n_ride, width), BF16),
            pltpu.SemaphoreType.DMA((SIDE,)),
        ],
        compiler_params=ROOMY,
        name="ride_sum",
    )(stack)


def give_copies(parts, other, sources, out_ref, sems):
    width = out_ref.shape[1]
    columns = pl.ds(pl.multiple_of(other * width, width), width)
    copies, at = [], 0
    for i, (which, row, n) in enumerate(parts):
        source = sources[which].at[pl.ds(row, n), columns]
        copies.append(pltpu.make_async_copy(source, out_ref.at[pl.ds(at, n)], sems.at[i]))
        copies[-1].start()
        at += n
    return copies


def give_kernel(parts, core_ref, *refs):
    sources, (out_ref, sems) = refs[:-2], refs[-2:]
    for copy in give_copies(parts, 1 - core_ref[0], sources, out_ref, sems):
        copy.wait()


def give_half(core, arrays, rows):
    any_spec = pl.BlockSpec(memory_space=pl.ANY)
    parts = [(i, at, rows) for i, a in enumerate(arrays) for at in range(0, a.shape[0], rows)]
    return pl.pallas_call(
        functools.partial(give_kernel, parts),
        out_shape=jax.ShapeDtypeStruct((len(parts) * rows, arrays[0].shape[1] // 2), BF16),
        in_specs=[pl.BlockSpec(memory_space=pltpu.SMEM)] + [any_spec] * len(arrays),
        out_specs=pl.BlockSpec(memory_space=pltpu.VMEM),
        scratch_shapes=[pltpu.SemaphoreType.DMA((len(parts),))],
        compiler_params=ROOMY,
        name="give",
    )(core, *arrays)


def give_near_kernel(parts, at_ride, place_ref, quarter_ref, *refs):
    sources, (out_ref, sums_ref, rides, sems) = refs[:-4], refs[-4:]
    copies = give_copies(parts, 1 - place_ref[0], sources, out_ref, sems)
    for k, far in enumerate(sources[-3:]):
        ride = far.at[pl.ds(at_ride, rides.shape[1])]
        copies.append(pltpu.make_async_copy(ride, rides.at[k], sems.at[len(parts) + k]))
        copies[-1].start()
    n = quarter_ref.shape[0]
    sums_ref[pl.ds(pl.multiple_of(place_ref[1] * n, n), n)] = quarter_ref[...]
    for copy in copies:
        copy.wait()
    for k in range(3):
        source = (place_ref[1] + SIDE - 1 - k) % SIDE
        ride = jnp.concatenate(jnp.split(rides[k], SIDE, axis=1), axis=0)
        sums_ref[pl.ds(pl.multiple_of(source * n, n), n)] = ride
    at = sum(part[2] for part in parts)
    out_ref[at:] = jnp.concatenate(jnp.split(sums_ref[...], 2, axis=0), axis=1)


def give_near(place, quarter, arrays, steps, rows):
    width = arrays[0].shape[1]
    at_ride = arrays[-1].shape[0] // rows * rows
    n_ride = arrays[-1].shape[0] - at_ride
    n, columns = quarter.shape
    parts = [
        (i, at, rows)
        for i, (a, step) in enumerate(zip(arrays, steps))
        for at in range(0, a.shape[0] - rows + 1, step)
    ]
    vmem, any_spec = pl.BlockSpec(memory_space=pltpu.VMEM), pl.BlockSpec(memory_space=pl.ANY)
    n_sums = SIDE * n * columns * 2 // width
    return pl.pallas_call(
        functools.partial(give_near_kernel, parts, at_ride),
        out_shape=(
            jax.ShapeDtypeStruct((len(parts) * rows + n_sums, width // 2), BF16),
            jax.ShapeDtypeStruct((SIDE * n, columns), BF16),
        ),
        in_specs=[pl.BlockSpec(memory_space=pltpu.SMEM), vmem] + [any_spec] * len(arrays),
        out_specs=(vmem,) * 2,
        scratch_shapes=[
            pltpu.VMEM((3, n_ride, width), BF16),
            pltpu.SemaphoreType.DMA((len(parts) + 3,)),
        ],
        compiler_params=ROOMY,
        name="give_near",
    )(place, quarter, *arrays)


def frozen_kernel(n_held, parts, core_ref, place_ref, *refs):
    sources, (mine, other, own, came, sems) = refs[:-5], refs[-5:]
    rows, cols = mine.shape
    blocks = len(parts) // 2
    width = own.shape[1] // blocks
    columns = pl.ds(pl.multiple_of(core_ref[0] * width, width), width)
    copies = []
    for i, (which, row) in enumerate(parts):
        if i < blocks:
            target = own.at[:, pl.ds(i * width, width)]
        else:
            at = pl.multiple_of(place_ref[i - blocks] * width, width)
            target = came.at[:, pl.ds(at, width)]
        source = sources[which].at[pl.ds(row, rows), columns if which < n_held else pl.ds(0, width)]
        copies.append(pltpu.make_async_copy(source, target, sems.at[i]))
    for copy in copies[blocks:] + copies[:blocks]:
        copy.start()
    for copy in copies[blocks:]:
        copy.wait()
    together = blocks // 4

    def total(first, second):
        result = None
        for i in range(0, blocks, together):
            for copy in copies[i : i + together]:
                copy.wait()
            depth = slice(i * width, (i + together) * width)
            term = lax.dot_general(
                first[:, depth], second[:, depth], NT, preferred_element_type=F32
            )
            result = term if result is None else result + term
        return result

    @pl.when(core_ref[0] == 0)
    def _():
        product = total(own, came)
        mine[...] = product[:, :cols]
        other[...] = product[:, cols:]

    @pl.when(core_ref[0] == 1)
    def _():
        product = total(came, own)
        mine[...] = product[:, cols:]
        other[...] = product[:, :cols]


def frozen_product(core, place, own, came, rows):
    arrays = [a for a, _ in (*own, *came)]
    parts = []
    for i, (a, step) in enumerate((*own, *came)):
        parts += [(i, at) for at in range(0, a.shape[0] - rows + 1, step)]
    width = came[0][0].shape[1]
    held = pltpu.VMEM((rows, len(parts) // 2 * width), BF16)
    return pl.pallas_call(
        functools.partial(frozen_kernel, len(own), parts),
        out_shape=(jax.ShapeDtypeStruct((rows, rows // 2), F32),) * 2,
        in_specs=[pl.BlockSpec(memory_space=pltpu.SMEM)] * 2
        + [pl.BlockSpec(memory_space=pl.ANY)] * len(arrays),
        out_specs=(pl.BlockSpec(memory_space=pltpu.VMEM),) * 2,
        scratch_shapes=[held, held, pltpu.SemaphoreType.DMA((len(parts),))],
        compiler_params=pltpu.CompilerParams(vmem_limit_bytes=56 * 1024 * 1024),
        cost_estimate=pl.CostEstimate(
            flops=4 * rows * rows * held.shape[1], bytes_accessed=24 << 20, transcendentals=0
        ),
        name="frozen",
    )(core, place, *arrays)


def block_order(core, dp, tensor):
    stage = jnp.array([0] * 4 + [1, 2] * 4 + [3] * 4, jnp.int32)
    step = jnp.array([0, 1, 2, 3, 0, 0, 1, 1, 2, 2, 3, 3, 0, 1, 2, 3], jnp.int32)
    first = core == 0
    mine, theirs = jnp.where(first, tensor, dp) // SIDE, jnp.where(first, dp, tensor) // SIDE
    high = jnp.where(stage == 0, step, (mine - step) % SIDE)
    shift = jnp.where(stage == 2, 3, jnp.where(stage == 3, 2, stage))
    low = jnp.where(first, (tensor - shift) % SIDE, (dp % SIDE) ^ stage)
    back = (tensor - low) % SIDE
    back = jnp.where(back == 2, 3, jnp.where(back == 3, 2, back))
    stage = jnp.where(first, (dp % SIDE) ^ low, back)
    step = (theirs - high) % SIDE
    return jnp.where(
        stage == 0, high, jnp.where(stage == 3, 12 + step, 3 + stage + 2 * step)
    )


def window(i, rows):
    return max(i - 1, 0) * rows


def forward_kernel(
    scale, q_ref, label_ref, lower_ref, keys_ref, values_ref, rows_ref, taps_ref,
    upper_ref, slab_ref, band_ref, out_ref, inner_ref, k_ref, v_ref, give_ref, sems,
):
    head = k_ref.shape[1]
    n, n_taps, (rank, width) = rows_ref.shape[0], taps_ref.shape[0], upper_ref.shape
    at_upper = n + n_taps
    at_inner = at_upper + rank // 2
    core = lax.axis_index("draft")
    heads = q_ref.shape[1] // head
    kv_head = (lax.axis_index("tensor") * 2 + core) * heads // (QUERY_HEAD_COUNT // KVH)
    mine = pl.ds(pl.multiple_of(kv_head * head, head), head)

    def copy(i, source, target):
        return pltpu.make_async_copy(source, target, sems.at[i])

    seen = [copy(0, keys_ref.at[:, mine], k_ref), copy(1, values_ref.at[:, mine], v_ref)]
    given = [copy(2, taps_ref, give_ref.at[pl.ds(n, n_taps)])]
    for i in range(2):
        target = give_ref.at[pl.ds(at_upper, rank // 2), pl.ds(i * width, width)]
        given.append(copy(3 + i, upper_ref.at[pl.ds(i * (rank // 2), rank // 2)], target))
    for one in seen + given:
        one.start()

    @pl.when(core == 0)
    def _():
        copy(5, slab_ref, give_ref.at[pl.ds(0, n)]).start()

    @pl.when(core == 1)
    def _():
        copy(5, rows_ref, give_ref.at[pl.ds(0, n)]).start()

    for one in seen:
        one.wait()
    rows = band_ref.shape[2] // 2
    labels = label_ref[...].astype(F32)
    ahead = lax.broadcasted_iota(jnp.int32, (rows, 2 * rows), 0)
    ahead = ahead - lax.broadcasted_iota(jnp.int32, (rows, 2 * rows), 1)
    tiles = [(i, h) for i in range(q_ref.shape[0] // rows) for h in range(band_ref.shape[0])]
    scores = {}
    for i, h in tiles:
        at, low = i * rows, window(i, rows)
        scores[i, h] = lax.dot_general(
            q_ref[at : at + rows, h * head : (h + 1) * head],
            k_ref[low : low + 2 * rows],
            NT,
            preferred_element_type=F32,
        )
    allowed = {}
    for i in range(q_ref.shape[0] // rows):
        at, low = i * rows, window(i, rows)
        own = jnp.broadcast_to(labels[:, at : at + rows], (rows, rows)).T
        own = jnp.concatenate([own, own], axis=1)
        allowed[i] = (ahead >= low - at) & (own == labels[:, low : low + 2 * rows])
    probs = {}
    for i, h in tiles:
        masked = jnp.where(allowed[i], scores[i, h] * scale, -jnp.inf)
        raised = jnp.exp(masked - jnp.max(masked, axis=1, keepdims=True))
        probs[i, h] = raised / jnp.sum(raised, axis=1, keepdims=True)
    outs = {}
    for i, h in tiles:
        low = window(i, rows)
        outs[i, h] = jnp.dot(
            probs[i, h].astype(BF16), v_ref[low : low + 2 * rows], preferred_element_type=F32
        ).astype(BF16)
    for i, h in tiles:
        at = i * rows
        band_ref[h, at : at + rows] = probs[i, h]
        out_ref[at : at + rows, h * head : (h + 1) * head] = outs[i, h]
    inner = lax.dot_general(out_ref[...], lower_ref[...], NT, preferred_element_type=F32)
    inner_ref[...] = inner
    inner = jnp.split(inner.astype(BF16), 2 * width // rank, axis=0)
    give_ref[at_inner:] = jnp.concatenate(inner, axis=1)
    for one in given:
        one.wait()
    copy(5, rows_ref, give_ref.at[pl.ds(0, n)]).wait()


def forward(queries, labels, lower, keys, values, rows, taps, upper, slab):
    n, width = queries.shape
    heads, rank = width // HEAD_WIDTH, lower.shape[0]
    any_spec = pl.BlockSpec(memory_space=pl.ANY)
    vmem = pl.BlockSpec(memory_space=pltpu.VMEM)
    n_give = rows.shape[0] + taps.shape[0] + rank // 2 + n * rank // rows.shape[1]
    return pl.pallas_call(
        functools.partial(forward_kernel, HEAD_WIDTH**-0.5),
        out_shape=(
            jax.ShapeDtypeStruct((heads, n, 2 * SEGMENT_MOST), F32),
            jax.ShapeDtypeStruct((n, width), BF16),
            jax.ShapeDtypeStruct((n, rank), F32),
            jax.ShapeDtypeStruct((n, HEAD_WIDTH), BF16),
            jax.ShapeDtypeStruct((n, HEAD_WIDTH), BF16),
            jax.ShapeDtypeStruct((n_give, rows.shape[1]), BF16),
        ),
        in_specs=[vmem] * 3 + [any_spec] * 6,
        out_specs=(vmem,) * 6,
        scratch_shapes=[pltpu.SemaphoreType.DMA((6,))],
        name="attention",
    )(queries, labels, lower, keys, values, rows, taps, upper, slab)


def backward_kernel(
    scale, core_ref, mine_ref, came_ref, adapter_ref, lower_ref, band_ref, out_ref, q_ref, k_ref,
    v_ref, query_ref, keep_ref, give_ref, key_sum, value_sum,
):
    rows = band_ref.shape[2] // 2
    head = k_ref.shape[1]
    n = q_ref.shape[0] // rows
    tiles = [(i, h) for i in range(n) for h in range(band_ref.shape[0])]

    def part(i):
        return slice(i * rows, (i + 1) * rows)

    def seen(i):
        return slice(window(i, rows), window(i, rows) + 2 * rows)

    def cols(h):
        return slice(h * head, (h + 1) * head)

    adapter = adapter_ref[:, lower_ref.shape[0] :]
    lora = jnp.dot(adapter, lower_ref[...], preferred_element_type=F32)
    gradient = (mine_ref[...] + came_ref[...] + adapter_scale * lora).astype(BF16)
    own = {(i, h): gradient[part(i), cols(h)] for i, h in tiles}
    prob_grad, terms, score_grad = {}, {}, {}
    for i, h in tiles:
        prob_grad[i, h] = lax.dot_general(
            own[i, h], v_ref[seen(i)], NT, preferred_element_type=F32
        )
    for i, h in tiles:
        product = own[i, h].astype(F32) * out_ref[part(i), cols(h)].astype(F32)
        terms[i, h] = jnp.sum(product, axis=1, keepdims=True)
    probs = {(i, h): band_ref[h, part(i)] for i, h in tiles}
    for i, h in tiles:
        score_grad[i, h] = (probs[i, h] * (prob_grad[i, h] - terms[i, h])).astype(BF16)
    for i, h in tiles:
        query_grad = jnp.dot(score_grad[i, h], k_ref[seen(i)], preferred_element_type=F32)
        query_ref[part(i), cols(h)] = (scale * query_grad).astype(BF16)
    for j in range(n):
        sees = [(j, 0 if j == 0 else 1)] + [(i, 0) for i in (j + 1,) if i < n]
        key_total, value_total = None, None
        for i, side in sees:
            for h in range(band_ref.shape[0]):
                key_part = lax.dot_general(
                    q_ref[part(i), cols(h)], score_grad[i, h][:, part(side)], TN,
                    preferred_element_type=F32,
                )
                value_part = lax.dot_general(
                    own[i, h], probs[i, h][:, part(side)].astype(BF16), TN,
                    preferred_element_type=F32,
                )
                key_total = key_part if key_total is None else key_total + key_part
                value_total = value_part if value_total is None else value_total + value_part
        key_sum[:, part(j)] = key_total
        value_sum[:, part(j)] = value_total
    quarter = head // 4
    first = core_ref[0] == 0
    for source, factor, at in ((key_sum, scale, 0), (value_sum, None, 2 * quarter)):
        total = source[...] if factor is None else source[...] * factor
        for i in (0, 1):
            even = total[2 * i * quarter : (2 * i + 1) * quarter]
            odd = total[(2 * i + 1) * quarter : (2 * i + 2) * quarter]
            rows = slice(at + i * quarter, at + (i + 1) * quarter)
            keep_ref[rows] = jnp.where(first, even, odd)
            give_ref[rows] = jnp.where(first, odd, even)


def backward(core, mine, came, adapter, lower, band, out, queries, key_head, value_head):
    n, width = queries.shape
    half = jax.ShapeDtypeStruct((HEAD_WIDTH, n), F32)
    return pl.pallas_call(
        functools.partial(backward_kernel, HEAD_WIDTH**-0.5),
        out_shape=(jax.ShapeDtypeStruct((n, width), BF16), half, half),
        in_specs=[pl.BlockSpec(memory_space=pltpu.SMEM)]
        + [pl.BlockSpec(memory_space=pltpu.VMEM)] * 9,
        out_specs=(pl.BlockSpec(memory_space=pltpu.VMEM),) * 3,
        scratch_shapes=[pltpu.VMEM((HEAD_WIDTH, n), F32)] * 2,
        cost_estimate=pl.CostEstimate(
            flops=20 * n * width * 2 * SEGMENT_MOST, bytes_accessed=16 << 20, transcendentals=0
        ),
        compiler_params=ROOMY,
        name="attention_gradient",
    )(core, mine, came, adapter, lower, band, out, queries, key_head, value_head)


def quarters_kernel(chip_ref, keep_ref, came_ref, out_ref, give_ref):
    quarter = keep_ref.shape[0] // 4
    first = chip_ref[0] == 0
    for i in (0, 1):
        at = 2 * i * quarter
        even = keep_ref[at : at + quarter] + came_ref[at : at + quarter]
        odd = keep_ref[at + quarter : at + 2 * quarter] + came_ref[at + quarter : at + 2 * quarter]
        rows = slice(i * quarter, (i + 1) * quarter)
        out_ref[rows] = jnp.where(first, even, odd)
        give_ref[rows] = jnp.where(first, odd, even).astype(BF16)


def quarters_kept(chip, keep, came):
    n, width = keep.shape
    return pl.pallas_call(
        quarters_kernel,
        out_shape=(
            jax.ShapeDtypeStruct((n // 2, width), F32),
            jax.ShapeDtypeStruct((n // 2, width), BF16),
        ),
        in_specs=[pl.BlockSpec(memory_space=pltpu.SMEM)]
        + [pl.BlockSpec(memory_space=pltpu.VMEM)] * 2,
        out_specs=(pl.BlockSpec(memory_space=pltpu.VMEM),) * 2,
        compiler_params=ROOMY,
        name="quarters",
    )(chip, keep, came)


def on_device(
    rotated_queries,
    rotated_keys,
    stored_values,
    segment_labels,
    output_gradient,
    draft_loss_gradients,
    tapped_row_index,
    output_projector,
    lower_factor_weight,
    upper_factor_weight,
):
    seq_len = rotated_queries.shape[1]
    head_size = HEAD_WIDTH
    heads_dev = rotated_queries.shape[2] // head_size
    group_size = QUERY_HEAD_COUNT // KVH
    score_scale = head_size ** (-0.5)
    core = lax.axis_index("draft")
    tensor = lax.axis_index("tensor")
    dp = lax.axis_index("dp")
    upper_core = core == 1
    rank_index = tensor * 2 + core
    kv_head = rank_index * heads_dev // group_size
    width = output_projector.shape[1] // 2
    rank = lower_factor_weight.shape[1]

    core_ref = core.reshape(1)
    y = tensor // SIDE
    place = jnp.stack([core, y, kv_head]).astype(jnp.int32)
    rows, taps = output_gradient[0], draft_loss_gradients[0]
    queries, lower = rotated_queries[0], lower_factor_weight.T
    band, output_flattened, inner_piece, key_head, value_head, give = forward(
        queries,
        segment_labels,
        lower,
        rotated_keys[0],
        stored_values[0],
        rows,
        taps,
        upper_factor_weight,
        output_projector,
    )
    block, _, stacked = blend(
        place,
        tapped_row_index,
        rows,
        taps,
        upper_factor_weight,
        output_projector,
        swapped(give, "draft", 1),
        inner_piece,
    )
    z1, z2 = near_move(block, 1, 1), near_move(block, 3, 2)

    half = seq_len // 2
    own_far = spread(stacked, AXES, far_groups())
    quarter = ride_sum(own_far, seq_len)
    from_z = [first_swapped(quarter, mask).astype(F32) for mask in (1, 2, 3)]
    quarter = ((quarter.astype(F32) + from_z[1]) + (from_z[0] + from_z[2])).astype(BF16)
    low = near_move(jnp.where(upper_core, block[:half], z1[:half]), 1, 3)
    high = near_move(jnp.where(upper_core, block[half:], z2[half:]), 3, 3)
    last = jnp.concatenate([low, high], axis=0)
    near = jnp.concatenate([z1, z2, widened(quarter, SIDE)], axis=0)
    near_far = in_step_order([far_move(near, k) for k in (2, 1, 3)])
    give, sums = give_near(
        place,
        after(quarter, last),
        [own_far, z1, z2, *near_far],
        [own_far.shape[0] // SIDE] + [seq_len] * 5,
        seq_len,
    )
    came_near = swapped(give, "draft", 1)
    residual = lax.dynamic_slice_in_dim(came_near, y * seq_len, seq_len, 0)
    residual = jnp.where(upper_core, residual, block[:, :width])
    last_far = in_step_order([far_move(last, k) for k in (2, 1, 3)])
    sums = jnp.where(upper_core, narrowed(came_near[12 * seq_len :], 2), sums)
    adapter_inner, adapter_gradient = sums[:, :rank], sums[:, rank:]

    lower_piece = lax.dot_general(adapter_gradient, output_flattened, TN, preferred_element_type=F32)
    upper_piece = lax.dot_general(adapter_inner, residual, TN, preferred_element_type=F32)
    factor = jnp.concatenate([lower_piece, upper_piece], axis=0)
    factor = factor + swapped(factor, "dp", 1)
    from_dp = swapped(factor, "dp", 2)
    give = give_half(core_ref, [after(last, came_near, factor), *last_far], seq_len)
    came_last = swapped(give, "draft", 1)

    part_mine, part_other = frozen_product(
        core_ref,
        block_order(1 - core, dp, tensor),
        [(own_far, own_far.shape[0] // SIDE)]
        + [(a, seq_len) for a in (z1, z2, *near_far, last, *last_far)],
        [(came_near, seq_len), (came_last, seq_len)],
        seq_len,
    )
    factor = factor + after(from_dp, part_mine)
    came = swapped(after(part_other, factor), "draft", 1)
    from_dp = swapped(factor, "dp", 4)
    query_grad, keep, give = backward(
        core_ref,
        part_mine,
        came,
        sums,
        lower,
        band,
        output_flattened,
        queries,
        key_head,
        value_head,
    )
    factor = factor + after(from_dp, give)
    came = swapped(after(give, factor), "draft", 1)
    from_dp = swapped(factor, "dp", 8)
    keep, give = quarters_kept((tensor & 1).reshape(1), keep, came)
    came = swapped(give, "tensor", 1)
    factor = factor + after(from_dp, give)
    factor = factor * (adapter_scale / lax.axis_size("dp"))
    lower_gradient, upper_gradient = factor[:rank].T, factor[rank:]
    total = (keep + came.astype(F32)).astype(BF16)
    quarter = head_size // 4
    key_grad, value_grad = total[:quarter].T[None], total[quarter:].T[None]
    query_grad = query_grad[None]
    return (query_grad, key_grad, value_grad, lower_gradient, upper_gradient)


def solution(mesh):
    in_specs = (
        P("dp", None, ("tensor", "draft")),
        P("dp", None, None),
        P("dp", None, None),
        P("dp", None),
        P("dp", "draft", "tensor"),
        P("dp", "draft", "tensor"),
        P("dp", None),
        P(("tensor", "draft"), "dp"),
        P(("tensor", "draft"), None),
        P(None, ("tensor", "draft")),
    )
    out_specs = (
        P("dp", None, ("tensor", "draft")),
        P("dp", None, ("tensor", "draft")),
        P("dp", None, ("tensor", "draft")),
        P(("tensor", "draft"), None),
        P(None, ("tensor", "draft")),
    )
    return jax.shard_map(
        on_device, mesh=mesh, in_specs=in_specs, out_specs=out_specs, check_vma=False
    )
```
